256 devices in a mesh: dp: 64 (over z, y, core), mp: 4 (over x).
Axes of the slice: x: 4, y: 4, z: 8, core: 2. Of those that a mesh axis runs over, the one named last changes fastest.
Arguments:
- queries: bfloat16 [16384, 4096], P('dp', 'mp'), may hold values from -160 to 160
- passages: bfloat16 [32768, 4096], P('dp', 'mp'), may hold values from -20 to 20
- pos_ids: int32 [512], P('dp'), may hold values from 0 to 1023, as said below
- neg_ids: int32 [512, 7], P('dp'), may hold values from -1 to 1023, as said below
- counts: int32 [512], P('dp'), may hold values from 1 to 7, as said below
Outputs:
- loss_rows: float32 [16384], P('dp')
- query_grad: bfloat16 [16384, 4096], P('dp', 'mp')
- passage_grad: bfloat16 [32768, 4096], P('dp', 'mp')
The draws below stay inside these ranges and needn't reach their ends.
Inputs may be any that keep to these rules, and one draw needn't show every extreme that they name: `pos_ids`: block g belongs to the index g // 16 of dp. Within the 8 query blocks of one index of dp, the positives and live negatives never name two different blocks of the same index of dp; within one query block they name distinct indices of dp. `neg_ids`: slots at counts and beyond hold -1; live slots name passage blocks. `counts`: some query block has 7 live slots in every draw.
All inputs are finite; a program needn't handle non-finite values.
Results may differ from the reference program's by a relative error of at most 0.011.
Values may be sent and summed in bfloat16 or wider, within the bound.
A program may use at most 128 MiB of HBM per device.

```python
import jax
import jax.numpy as jnp
from jax import lax

D = 4096
BR = 32
K = 7
PB = 16
QB = 8
NQB = 512
NPB = 1024
NQ = 16384
NP = 32768


def candidate_lists(key):
    owners = NQB // QB
    assign_key, order_key, count_key, heavy_key = jax.random.split(key, 4)
    assigned = jax.random.randint(assign_key, (owners, owners), 0, PB)
    assigned = assigned.at[0, owners - 1].set(PB - 1)
    noise = jax.random.randint(order_key, (NQB, owners), 0, 1 << 20) * owners + jnp.arange(owners)[None, :]
    noise = noise.at[0, owners - 1].set(-1)
    order = jnp.argsort(noise, axis=1)[:, :K + 1].astype(jnp.int32)
    home = jnp.arange(NQB) // QB
    blocks = order * PB + assigned[home[:, None], order]
    live_counts = jax.random.randint(count_key, (NQB,), 1, K + 1)
    heavy = jax.random.randint(heavy_key, (), 1, NQB)
    live_counts = live_counts.at[0].set(1).at[heavy].set(K)
    negatives = jnp.where(jnp.arange(K)[None, :] < live_counts[:, None], blocks[:, 1:], -1)
    return (blocks[:, 0].astype(jnp.int32), negatives.astype(jnp.int32), live_counts.astype(jnp.int32))


def passage_bank(key):
    base = jnp.clip(jax.random.normal(jax.random.fold_in(key, 101), (NP, D), jnp.float32), -5.0, 5.0)
    return base


def draw_pos_ids(key, part):
    lists = candidate_lists(key)
    return lists[0]


def draw_neg_ids(key, part):
    lists = candidate_lists(key)
    return lists[1]


def draw_counts(key, part):
    lists = candidate_lists(key)
    return lists[2]


def draw_passages(key, part):
    bank = passage_bank(key)
    return bank.astype(jnp.bfloat16)


def draw_queries(key, part):
    key = jax.random.fold_in(key, 5)
    base = jnp.clip(jax.random.normal(key, (NQ, D), jnp.float32), -5.0, 5.0)
    return base.astype(jnp.bfloat16)


def setup_inputs(seed: int = 0) -> dict:
    seeds = jax.random.split(jax.random.key(seed), 6)
    return {
        "queries": draw_queries(jax.random.fold_in(seeds[5], 71), 0),
        "passages": draw_passages(jax.random.fold_in(seeds[5], 71), 0),
        "pos_ids": draw_pos_ids(jax.random.fold_in(seeds[5], 71), 0),
        "neg_ids": draw_neg_ids(jax.random.fold_in(seeds[5], 71), 0),
        "counts": draw_counts(jax.random.fold_in(seeds[5], 71), 0),
    }


def reference(queries, passages, pos_ids, neg_ids, counts):
    slot_count = K + 1
    inverse_temp = D ** -0.5
    passage_tiles = passages.reshape(NPB, BR, D)
    query_tiles = queries.reshape(NQB, BR, D)
    alive_slots = jnp.concatenate([jnp.ones((NQB, 1), bool), jnp.arange(K)[None, :] < counts[:, None]], axis=1)
    candidates = jnp.where(alive_slots, jnp.concatenate([pos_ids[:, None], neg_ids], axis=1), 0).astype(jnp.int32)
    target = (jnp.arange(slot_count) == 0)[None, :, None] & jnp.eye(BR, dtype=bool)[:, None, :]

    def one_block(carry, inputs):
        tile, chosen, alive = inputs
        picked = passage_tiles[chosen].astype(jnp.float32)
        wide_tile = tile.astype(jnp.float32)
        scores = jnp.einsum("rd,kcd->rkc", wide_tile, picked) * inverse_temp
        logits = jnp.where(alive[None, :, None], scores, -1e30)
        row_max = jnp.max(logits, axis=(1, 2), keepdims=True)
        exp_terms = jnp.exp(logits - row_max)
        row_total = jnp.sum(exp_terms, axis=(1, 2), keepdims=True)
        log_total = row_max + jnp.log(row_total)
        block_loss = log_total[:, 0, 0] - jnp.sum(jnp.where(target, logits, 0.0), axis=(1, 2))
        weights = (exp_terms / row_total - target.astype(jnp.float32)).astype(jnp.bfloat16)
        wide_weights = weights.astype(jnp.float32)
        block_grad = jnp.einsum("rkc,kcd->rd", wide_weights, picked).astype(jnp.bfloat16)
        panel_terms = jnp.einsum("rkc,rd->kcd", wide_weights, wide_tile)
        carry = carry.at[chosen].add(panel_terms)
        return carry, (block_loss, block_grad)

    start_grad = jnp.zeros((NPB, BR, D), jnp.float32)
    total_grad, (loss_rows, query_grad) = lax.scan(one_block, start_grad, (query_tiles, candidates, alive_slots))
    return loss_rows.reshape(NQ), query_grad.reshape(NQ, D), total_grad.reshape(NP, D).astype(jnp.bfloat16)
```

```python
import jax
import jax.numpy as jnp
from jax import lax
from jax.experimental import pallas as pl
from jax.experimental.pallas import tpu as pltpu
from jax.sharding import PartitionSpec as P

D = 4096
BR = 32
NZ, NY, NC, NX = 8, 4, 2, 4
RY = (0, 1, 3, 2)
W = 1024
QR = 256
PR = 512
MESH = pl.DeviceIdType.MESH
F32 = jnp.float32
BF16 = jnp.bfloat16


def index_of(dy, dc):
    return RY.index(dy % NY) * NC + dc


def dot(a, b, ca, cb):
    return lax.dot_general(a, b, (((ca,), (cb,)), ((), ())), preferred_element_type=F32)


def kernel(cand_ref, q_hbm, p_hbm, loss_ref, qg_ref, pg_ref,
           qb, pb, psel, bsel, meta, sels, selt, codes, sb, srv, lg, stcol, stat, tot, wb, lossb,
           gf, gsp, gsm, grp, grm, pn, rb, acc,
           lsem, qs, qr, ps, pr, sibs, sibr, ms, mr, es, er, ss, sr, ts, tr, ws, wr, ls, lr, gs, gr, ns, nr):
    dp = lax.axis_index("dp")
    x = lax.axis_index("mp")
    z = dp // (NY * NC)
    y = lax.rem(dp // NC, NY)
    c = lax.rem(dp, NC)

    def dev(dz=0, dy=0, dc=0, dx=0):
        there = lax.rem(z + dz, NZ) * (NY * NC) + lax.rem(y + dy, NY) * NC + lax.rem(c + dc, NC)
        return (there, lax.rem(x + dx, NX))

    row = [(RY[o // NC], o % NC) for o in range(8)]
    peers = [dev(dz=d) for d in range(1, NZ)] + [dev(dy=a, dc=b) for a, b in row[1:]] + [dev(dx=d) for d in range(1, NX)]
    barrier = pltpu.get_barrier_semaphore()
    for p in peers:
        pl.semaphore_signal(barrier, 1, device_id=p, device_id_type=MESH)

    load_q = pltpu.make_async_copy(q_hbm, qb.at[0], lsem.at[0])
    load_p = pltpu.make_async_copy(p_hbm, pb.at[0, 0], lsem.at[1])
    load_q.start()
    load_p.start()

    sent = []

    def send(src, dst, ssem, rsem, to):
        cp = pltpu.make_async_remote_copy(src_ref=src, dst_ref=dst, send_sem=ssem, recv_sem=rsem, device_id=to, device_id_type=MESH)
        cp.start()
        sent.append(cp)

    def arrived(dst, rsem):
        pltpu.make_async_remote_copy(src_ref=dst, dst_ref=dst, send_sem=rsem, recv_sem=rsem, device_id=peers[0],
                                     device_id_type=MESH).wait_recv()

    lane = lax.broadcasted_iota(jnp.int32, (8, 128), 1)
    o_l = lane & 7
    og = o_l >> 1
    ry_l = og ^ (og >> 1)
    owner = (((z + (lane >> 3)) & 7) << 3) + (((y + ry_l) & 3) << 1) + (c ^ (o_l & 1))
    owner = jnp.where(lane < 64, owner, -7)
    code = jnp.zeros((8, 128), jnp.int32)
    sel = jnp.full((8, 128), -1, jnp.int32)
    for s in range(8):
        col = jnp.broadcast_to(cand_ref[:, s:s + 1], (8, 128))
        hit = (col >= 0) & ((col >> 4) == owner)
        code = jnp.where(hit, 2 if s == 0 else 1, code)
        sel = jnp.where(hit, col & 15, sel)
    sel = jnp.broadcast_to(jnp.max(sel, axis=0, keepdims=True), (8, 128))
    meta[0] = jnp.concatenate([code, sel], axis=0).astype(F32).astype(BF16)

    load_q.wait()
    load_p.wait()
    pl.semaphore_wait(barrier, len(peers))

    for d in range(1, NZ):
        send(meta.at[0], meta.at[8 - d], ms.at[d - 1], mr.at[7 - d], dev(dz=d))

    def rows(i, n=64):
        return pl.ds(i * n, n)

    def send_q(t):
        h = t // 4
        ip, im = t % 4, t % 4 + (2 if h == 3 else 0)
        send(qb.at[(8 - h) % 8, rows(ip)], qb.at[7 - h, rows(ip)], qs.at[0, t], qr.at[0, t], dev(dz=1))
        send(qb.at[h, rows(im)], qb.at[h + 1, rows(im)], qs.at[1, t], qr.at[1, t], dev(dz=NZ - 1))

    def p_part(t):
        if t < 8:
            return t, (t + 4) % 8
        return t - 8, t - 4

    def send_p(t):
        ip, im = p_part(t)
        a, b = ((0, 3), (0, 1)) if t < 8 else ((3, 2), (1, 2))
        send(pb.at[a[0], 0, rows(ip)], pb.at[a[1], 0, rows(ip)], ps.at[0, t], pr.at[0, t], dev(dy=1))
        send(pb.at[b[0], 0, rows(im)], pb.at[b[1], 0, rows(im)], ps.at[1, t], pr.at[1, t], dev(dy=NY - 1))

    def send_sib(a, half):
        k = 2 * a + half
        send(pb.at[a, 0, rows(half, 256)], pb.at[a, 1, rows(half, 256)], sibs.at[k], sibr.at[k], dev(dc=1))

    def sib_arrived(a):
        for half in range(2):
            k = 2 * a + half
            arrived(pb.at[a, 1, rows(half, 256)], sibr.at[k])

    for t in range(4):
        send_q(t)
        send_p(t)
    for t in range(4, 8):
        send_p(t)
    send_sib(0, 0)
    send_sib(0, 1)

    for r in range(1, NZ):
        arrived(meta.at[r], mr.at[r - 1])
    sub16 = lax.broadcasted_iota(jnp.int32, (16, 128), 0)
    rowc = lax.broadcasted_iota(jnp.int32, (8, 128), 0)
    table = jnp.zeros((16, 128), F32)
    for r in range(NZ):
        t = (8 - r) % 8
        tile = meta[r]
        wide = tile.astype(F32)
        own = wide[8:16]
        pair = jnp.concatenate([own, own], axis=0)
        table = jnp.where(sub16 == r, pair, table)
        for k in range(4):
            selt[r, pl.ds(8 * k, 8), :] = own * 32.0 + (rowc + 8 * k).astype(F32)
        spread = (lax.broadcasted_iota(jnp.int32, (128, QR), 0)
                  == t * 8 + (lax.broadcasted_iota(jnp.int32, (128, QR), 1) >> 5))
        codes[r] = dot(tile, spread.astype(F32).astype(BF16), 1, 0)
    sels[0] = table.astype(BF16)
    for o in range(1, 8):
        dy, dc = row[o]
        back = index_of(-dy, dc)
        send(sels.at[0], sels.at[back], es.at[o - 1], er.at[back - 1], dev(dy=dy, dc=dc))

    jl = lax.broadcasted_iota(jnp.int32, (BR, PR), 1).astype(F32)

    def pick(o):
        dy, dc = row[o]
        for r in range(NZ):
            k = ((8 - r) % 8) * 8 + o
            want = jnp.broadcast_to(selt[r, :, k:k + 1], (BR, PR))
            bsel[pl.ds(r * BR, BR), :] = (want == jl).astype(F32).astype(BF16)

        def part(n, _):
            cols = pl.ds(pl.multiple_of(n * 256, 256), 256)
            got = dot(bsel[...], pb[dy, dc, :, cols], 1, 0).astype(BF16)
            for r in range(NZ):
                psel[r, pl.ds(o * BR, BR), cols] = got[r * BR:(r + 1) * BR]
            return 0

        lax.fori_loop(0, 4, part, 0)

    def score(r, half):
        sb[r, half] = dot(qb[r], psel[r, pl.ds(half * 128, 128), :], 1, 1)
        for d in range(1, NX):
            xt = lax.rem(x + d, NX)
            send(sb.at[r, half, pl.ds(pl.multiple_of(xt * 64, 64), 64)], srv.at[r, half, 3 - d],
                 ss.at[r, half, d - 1], sr.at[r, half, 3 - d], dev(dx=d))

    mine = pl.ds(pl.multiple_of(x * 64, 64), 64)
    lane256 = lax.broadcasted_iota(jnp.int32, (64, QR), 1)
    row256 = lax.broadcasted_iota(jnp.int32, (64, QR), 0)
    same_row = (lane256 & 31) == (row256 & 31)
    lane64 = lax.broadcasted_iota(jnp.int32, (64, 128), 1)

    def asked(r):
        two = [jnp.broadcast_to(codes[r, pl.ds(2 * x + k, 1), :], (BR, QR)) for k in range(2)]
        return jnp.concatenate(two, axis=0)

    def home_rows(r):
        return pl.ds(pl.multiple_of(lax.rem(z + r, NZ) * 64, 64), 64)

    def row_stats(r):
        for half in range(2):
            for k in range(3):
                arrived(srv.at[r, half, k], sr.at[r, half, k])
        halves = [sb[r, half, mine, :] + srv[r, half, 0] + srv[r, half, 1] + srv[r, half, 2] for half in range(2)]
        summed = jnp.concatenate(halves, axis=1)
        ask = asked(r)
        live = ask > 0.5
        logits = jnp.where(live, summed * (D ** -0.5), -1e30)
        lg[r] = logits
        top = jnp.max(logits, axis=1, keepdims=True)
        total = jnp.sum(jnp.where(live, jnp.exp(logits - top), 0.0), axis=1, keepdims=True)
        pos = jnp.sum(jnp.where((ask > 1.5) & same_row, logits, 0.0), axis=1, keepdims=True)
        stcol[home_rows(r), :] = jnp.where(lane64 == 0, top, jnp.where(lane64 == 1, total, jnp.where(lane64 == 2, pos, 0.0)))

    pick(0)
    for t in range(14):
        h, i = t // 4, t % 4
        arrived(qb.at[7 - h, rows(i)], qr.at[0, t])
        arrived(qb.at[h + 1, rows(i + (2 if h == 3 else 0))], qr.at[1, t])
        if t < 8:
            send_q(t + 4)
        elif t < 10:
            u = t + 4
            send(qb.at[5, rows(t - 8)], qb.at[4, rows(t - 8)], qs.at[0, u], qr.at[0, u], dev(dz=1))
        elif t < 12:
            u = t + 2
            send(qb.at[3, rows(t - 8)], qb.at[4, rows(t - 8)], qs.at[1, u], qr.at[1, u], dev(dz=NZ - 1))
        if t < 12:
            ip, im = p_part(t)
            a, b = (3, 1) if t < 8 else (2, 2)
            arrived(pb.at[a, 0, rows(ip)], pr.at[0, t])
            arrived(pb.at[b, 0, rows(im)], pr.at[1, t])
            if t < 4:
                send_p(t + 8)
            if t == 3:
                send_sib(3, 0)
                send_sib(1, 1)
            if t == 7:
                send_sib(3, 1)
                send_sib(1, 0)
            if t == 11:
                send_sib(2, 0)
                send_sib(2, 1)
        if t == 0:
            sib_arrived(0)
            pick(1)
        if t == 7:
            pick(2)
        if t == 8:
            sib_arrived(1)
            pick(3)
            for r in (0, 1, 7, 2, 6):
                score(r, 0)
        if t == 9:
            pick(4)
        if t == 10:
            sib_arrived(3)
            pick(5)
        if t == 11:
            score(3, 0)
            score(5, 0)
            pick(6)
        if t == 12:
            sib_arrived(2)
            pick(7)
            for r in (0, 1, 7, 2, 6, 3, 5):
                score(r, 1)
    score(4, 0)
    score(4, 1)
    for r in (0, 1, 7, 2, 6, 3, 5, 4):
        row_stats(r)

    stat[0] = jnp.transpose(stcol[...])[0:8]
    for d in range(1, NZ):
        send(stat.at[0], stat.at[8 - d], ts.at[d - 1], tr.at[7 - d], dev(dz=d))
    for d in range(1, NZ):
        arrived(stat.at[d], tr.at[d - 1])
    top = stat[0, 0:1]
    for d in range(1, NZ):
        top = jnp.maximum(top, stat[d, 0:1])
    total = jnp.zeros((1, 512), F32)
    pos = jnp.zeros((1, 512), F32)
    for d in range(NZ):
        total = total + stat[d, 1:2] * jnp.exp(stat[d, 0:1] - top)
        pos = pos + stat[d, 2:3]
    loss = (top - pos) + jnp.log(total)
    sub = lax.broadcasted_iota(jnp.int32, (128, 512), 0)
    both = jnp.where(sub < 64, jnp.broadcast_to(top, (128, 512)), jnp.broadcast_to(1.0 / total, (128, 512)))
    tot[...] = jnp.transpose(both)
    loss8 = jnp.broadcast_to(loss, (8, 512))
    tile = jnp.zeros((8, 128), F32)
    for k in range(4):
        tile = jnp.where(z // 2 == k, loss8[:, k * 128:(k + 1) * 128], tile)
    lossb[x] = tile
    for d in range(1, NX):
        send(lossb.at[x], lossb.at[x], ls.at[d - 1], lr.at[3 - d], dev(dx=d))

    order = (4, 3, 5, 2, 6, 1, 7, 0)

    def weigh(r):
        both = tot[home_rows(r), :]
        top = jnp.broadcast_to(both[:, 0:1], (64, QR))
        inv = jnp.broadcast_to(both[:, 64:65], (64, QR))
        hot = jnp.where((asked(r) > 1.5) & same_row, 1.0, 0.0)
        wb[r, mine, :] = (jnp.exp(lg[r] - top) * inv - hot).astype(BF16)
        for d in range(1, NX):
            send(wb.at[r, mine], wb.at[r, mine], ws.at[r, d - 1], wr.at[r, 3 - d], dev(dx=d))

    for r in order:
        weigh(r)

    def panels(r):
        def part(n, _):
            cols = pl.ds(pl.multiple_of(n * 256, 256), 256)
            pn[r, :, cols] = dot(wb[r], qb[r, :, cols], 0, 0).astype(BF16)
            return 0

        lax.fori_loop(0, 4, part, 0)
        for o in range(1, 8):
            dy, dc = row[o]
            back = index_of(-dy, dc)
            send(pn.at[r, pl.ds(o * BR, BR)], rb.at[r, pl.ds(back * BR, BR)], ns.at[r, o - 1], nr.at[r, back - 1],
                 dev(dy=dy, dc=dc))
        rb[r, pl.ds(0, BR), :] = pn[r, pl.ds(0, BR), :]

    def grads(r):
        def part(n, _):
            cols = pl.ds(pl.multiple_of(n * 256, 256), 256)
            gf[r, :, cols] = dot(wb[r], psel[r, :, cols], 1, 0)
            return 0

        lax.fori_loop(0, 4, part, 0)

    def weights_arrived(r):
        for d in range(1, NX):
            other = pl.ds(pl.multiple_of(lax.rem(x + d, NX) * 64, 64), 64)
            arrived(wb.at[r, other], wr.at[r, d - 1])

    def pass_on(side, h, i, add):
        mineb, came = (gsp, grp) if side == 0 else (gsm, grm)
        r = 4 - h if side == 0 else (4 + h) % 8
        value = gf[r, rows(i), :]
        if add:
            arrived(came.at[h - 1, rows(i)], gr.at[side, h - 1, i])
            value = value + came[h - 1, rows(i), :].astype(F32)
        mineb[h, rows(i), :] = value.astype(BF16)
        send(mineb.at[h, rows(i)], came.at[h, rows(i)], gs.at[side, h, i], gr.at[side, h, i],
             dev(dz=1 if side == 0 else NZ - 1))

    weights_arrived(4)
    grads(4)
    for k in range(2):
        pass_on(0, 0, k, False)
        pass_on(1, 0, 2 + k, False)
    panels(4)
    for h in range(1, 4):
        for r in (4 - h, 4 + h):
            weights_arrived(r)
            grads(r)
            if h == 1:
                for k in range(2):
                    pass_on(0 if r == 3 else 1, 1, (2 + k) if r == 3 else k, False)
            panels(r)
        for k in range(4):
            if h == 1 and k < 2:
                continue
            pass_on(0, h, (k + 2) % 4, True)
            pass_on(1, h, k, True)
    weights_arrived(0)
    grads(0)
    panels(0)

    for o in range(1, 8):
        arrived(sels.at[o], er.at[o - 1])

    def collect(r, first):
        for j in range(1, 8):
            arrived(rb.at[r, pl.ds(j * BR, BR)], nr.at[r, j - 1])
        rowb = lax.broadcasted_iota(jnp.int32, (BR, PR), 0).astype(F32)
        for j in range(8):
            dy, dc = row[j]
            k = ((8 - r) % 8) * 8 + index_of(-dy, dc)
            line = sels[j].astype(F32)[r:r + 1, k:k + 1]
            want = jnp.broadcast_to(line, (BR, PR)) * 32.0 + rowb
            bsel[pl.ds(j * BR, BR), :] = (want == jl).astype(F32).astype(BF16)

        def part(n, _):
            cols = pl.ds(pl.multiple_of(n * 256, 256), 256)
            term = dot(bsel[...], rb[r, :, cols], 0, 0)
            acc[:, cols] = term if first else acc[:, cols] + term
            return 0

        lax.fori_loop(0, 4, part, 0)

    for n, r in enumerate(order[:-1]):
        collect(r, n == 0)
    for k in range(4):
        ip, im = (k + 2) % 4, k
        arrived(grp.at[3, rows(ip)], gr.at[0, 3, ip])
        arrived(grm.at[3, rows(im)], gr.at[1, 3, im])
    for k in range(4):
        qg_ref[rows(k), :] = (gf[0, rows(k), :] + grp[3, rows(k), :].astype(F32) + grm[3, rows(k), :].astype(F32)).astype(BF16)
    for d in range(1, NX):
        other = lax.rem(x + d, NX)
        arrived(lossb.at[other], lr.at[d - 1])
    low = lax.broadcasted_iota(jnp.int32, (8, 128), 1) < 64
    odd = lax.rem(z, 2) == 1
    for k in range(2):
        a, b = lossb[2 * k], lossb[2 * k + 1]
        even_case = jnp.where(low, a, pltpu.roll(b, 64, 1))
        odd_case = jnp.where(low, pltpu.roll(a, 64, 1), b)
        loss_ref[k:k + 1, :] = jnp.where(odd, odd_case, even_case)[0:1]
    collect(0, False)
    for k in range(8):
        pg_ref[rows(k), :] = acc[rows(k), :].astype(BF16)
    for cp in sent:
        cp.wait_send()


def body(queries, passages, pos_ids, neg_ids, counts):
    slots = neg_ids.shape[1]
    live = jnp.arange(slots)[None, :] < counts[:, None]
    cand = jnp.concatenate([pos_ids[:, None], jnp.where(live, neg_ids, -1)], axis=1)
    dma = pltpu.SemaphoreType.DMA
    vm = pltpu.VMEM
    loss, query_grad, passage_grad = pl.pallas_call(
        kernel,
        out_shape=(jax.ShapeDtypeStruct((2, 128), F32), jax.ShapeDtypeStruct((QR, W), BF16), jax.ShapeDtypeStruct((PR, W), BF16)),
        in_specs=[pl.BlockSpec(memory_space=pltpu.VMEM), pl.BlockSpec(memory_space=pl.ANY), pl.BlockSpec(memory_space=pl.ANY)],
        out_specs=tuple([pl.BlockSpec(memory_space=pltpu.VMEM)] * 3),
        scratch_shapes=[
            vm((8, QR, W), BF16), vm((NY, NC, PR, W), BF16), vm((8, QR, W), BF16), vm((QR, PR), BF16),
            vm((8, 16, 128), BF16), vm((8, 16, 128), BF16), vm((8, BR, 128), F32), vm((8, 16, QR), F32),
            vm((8, 2, QR, 128), F32), vm((8, 2, 3, 64, 128), F32), vm((8, 64, QR), F32), vm((512, 128), F32),
            vm((8, 8, 512), F32), vm((512, 128), F32), vm((8, QR, QR), BF16), vm((NX, 8, 128), F32),
            vm((8, QR, W), F32), vm((4, QR, W), BF16), vm((4, QR, W), BF16), vm((4, QR, W), BF16), vm((4, QR, W), BF16),
            vm((8, QR, W), BF16), vm((8, QR, W), BF16), vm((PR, W), F32),
            dma((2,)), dma((2, 14)), dma((2, 14)), dma((2, 12)), dma((2, 12)), dma((8,)), dma((8,)), dma((7,)), dma((7,)),
            dma((7,)), dma((7,)), dma((8, 2, 3)), dma((8, 2, 3)), dma((7,)), dma((7,)), dma((8, 3)), dma((8, 3)),
            dma((3,)), dma((3,)), dma((2, 4, 4)), dma((2, 4, 4)), dma((8, 7)), dma((8, 7)),
        ],
        compiler_params=pltpu.CompilerParams(collective_id=0, has_side_effects=True, vmem_limit_bytes=60 * 2**20),
        cost_estimate=pl.CostEstimate(flops=10**10, bytes_accessed=4 * 10**6, transcendentals=10**6),
    )(cand, queries, passages)
    return loss.reshape(QR), query_grad, passage_grad


def solution(mesh):
    assert mesh.shape["dp"] == NZ * NY * NC and mesh.shape["mp"] == NX
    return jax.shard_map(
        body,
        mesh=mesh,
        in_specs=(P("dp", "mp"), P("dp", "mp"), P("dp"), P("dp", None), P("dp")),
        out_specs=(P("dp"), P("dp", "mp"), P("dp", "mp")),
        check_vma=False,
    )
```

```python
import jax
import jax.numpy as jnp
from jax import lax
from jax.experimental import pallas as pl
from jax.experimental.pallas import tpu as pltpu
from jax.sharding import PartitionSpec as P

D = 4096
BR = 32
NZ, NY, NC, NX = 8, 4, 2, 4
RY = (0, 1, 3, 2)
W = 1024
QR = 256
PR = 512
MESH = pl.DeviceIdType.MESH
F32 = jnp.float32
BF16 = jnp.bfloat16


def index_of(dy, dc):
    return RY.index(dy % NY) * NC + dc


def dot(a, b, ca, cb):
    return lax.dot_general(a, b, (((ca,), (cb,)), ((), ())), preferred_element_type=F32)


def kernel(pos_ref, neg_ref, cnt_ref, q_hbm, p_hbm, loss_ref, qg_ref, pg_ref,
           qb, pb, psel, bsel, bback, meta, sels, selt, ask, st, srv, lg, stat, norm, wt, lossb,
           gf, gsp, gsm, grp, grm, pn, rb, acc,
           lsem, qs, qr, ps, pr, sibs, sibr, ms, mr, es, er, ss, sr, ts, tr, ws, wr, ls, lr, gs, gr, ns, nr):
    dp = lax.axis_index("dp")
    x = lax.axis_index("mp")
    z = dp // (NY * NC)
    y = lax.rem(dp // NC, NY)
    c = lax.rem(dp, NC)
    xm, xh = x // 2, lax.rem(x, 2)

    def dev(dz=0, dy=0, dc=0, dx=0):
        there = lax.rem(z + dz, NZ) * (NY * NC) + lax.rem(y + dy, NY) * NC + lax.rem(c + dc, NC)
        return (there, lax.rem(x + dx, NX))

    row = [(RY[o // NC], o % NC) for o in range(8)]
    peers = [dev(dz=d) for d in range(1, NZ)] + [dev(dy=a, dc=b) for a, b in row[1:]] + [dev(dx=d) for d in range(1, NX)]
    barrier = pltpu.get_barrier_semaphore()
    for p in peers:
        pl.semaphore_signal(barrier, 1, device_id=p, device_id_type=MESH)

    load_q = pltpu.make_async_copy(q_hbm, qb.at[0], lsem.at[0])
    load_p = pltpu.make_async_copy(p_hbm, pb.at[0, 0], lsem.at[1])
    load_q.start()
    load_p.start()

    sent = []

    def remote(src, dst, ssem, rsem, to):
        return pltpu.make_async_remote_copy(src_ref=src, dst_ref=dst, send_sem=ssem, recv_sem=rsem, device_id=to, device_id_type=MESH)

    def send(*args, when=None):
        if when is None:
            remote(*args).start()
        else:
            @pl.when(when)
            def _():
                remote(*args).start()
        sent.append((args, when))

    def arrived(dst, rsem):
        remote(dst, dst, rsem, rsem, peers[0]).wait_recv()

    def rows(i, n=64):
        return pl.ds(i * n, n)

    def send_q(k, j):
        i = k * 4 + j
        right, left = (q_hbm, q_hbm) if k == 0 else (qb.at[8 - k], qb.at[k])
        send(right.at[rows(j)], qb.at[7 - k, rows(j)], qs.at[0, i], qr.at[0, i], dev(dz=1))
        jm = (j + 2) % 4
        send(left.at[rows(jm)], qb.at[k + 1, rows(jm)], qs.at[1, i], qr.at[1, i], dev(dz=NZ - 1))

    def q_arrived(k, j):
        i = (k - 1) * 4 + j
        arrived(qb.at[8 - k, rows(j)], qr.at[0, i])
        arrived(qb.at[k, rows((j + 2) % 4)], qr.at[1, i])

    def p_part(t):
        if t < 8:
            return t, (t + 4) % 8
        return t - 8, t - 4

    def send_p(t):
        ip, im = p_part(t)
        up, down = (p_hbm, p_hbm) if t < 8 else (pb.at[3, 0], pb.at[1, 0])
        a, b = (3, 1) if t < 8 else (2, 2)
        send(up.at[rows(ip)], pb.at[a, 0, rows(ip)], ps.at[0, t], pr.at[0, t], dev(dy=1))
        send(down.at[rows(im)], pb.at[b, 0, rows(im)], ps.at[1, t], pr.at[1, t], dev(dy=NY - 1))

    def send_sib(a, i, n, k):
        send((p_hbm if a == 0 else pb.at[a, 0]).at[rows(i, n)], pb.at[a, 1, rows(i, n)], sibs.at[k], sibr.at[k], dev(dc=1))

    def sib_arrived(a):
        if a == 2:
            for i in range(8):
                arrived(pb.at[2, 1, rows(i)], sibr.at[8 + i])
        else:
            for half in range(2):
                arrived(pb.at[a, 1, rows(half, 256)], sibr.at[2 * a + half])

    lane = lax.broadcasted_iota(jnp.int32, (8, 128), 1)
    sub8 = lax.broadcasted_iota(jnp.int32, (8, 128), 0)
    o_l = lane & 7
    og = o_l >> 1
    ry_l = og ^ (og >> 1)
    owner = (((z + (lane >> 3)) & 7) << 3) + (((y + ry_l) & 3) << 1) + (c ^ (o_l & 1))
    owner = jnp.where(lane < 64, owner, -7)
    code = jnp.zeros((8, 128), jnp.int32)
    sel = jnp.full((8, 128), -1, jnp.int32)
    for s in range(8):
        col = jnp.full((8, 128), -1, jnp.int32)
        for b in range(8):
            block = pos_ref[b] if s == 0 else jnp.where(s - 1 < cnt_ref[b], neg_ref[b, s - 1], -1)
            col = jnp.where(sub8 == b, block, col)
        hit = (col >= 0) & ((col >> 4) == owner)
        code = jnp.where(hit, 2 if s == 0 else 1, code)
        sel = jnp.where(hit, col & 15, sel)
    sel = jnp.broadcast_to(jnp.max(sel, axis=0, keepdims=True), (8, 128))
    meta[0] = jnp.concatenate([code, sel], axis=0).astype(F32).astype(BF16)
    pl.semaphore_wait(barrier, len(peers))
    for d in range(1, NZ):
        send(meta.at[0], meta.at[8 - d], ms.at[d - 1], mr.at[7 - d], dev(dz=d))
    for j in range(4):
        send_q(0, j)
        send_p(j)
    for t in range(4, 8):
        send_p(t)
    send_sib(0, 0, 256, 0)
    send_sib(0, 1, 256, 1)

    def my_home(p):
        return lax.rem(p + 4 * xm - z + 8, 8)

    def take_lists():
        for r in range(1, NZ):
            arrived(meta.at[r], mr.at[r - 1])
        sub16 = lax.broadcasted_iota(jnp.int32, (16, 128), 0)
        table = jnp.zeros((16, 128), F32)
        for r in range(NZ):
            own = meta[r].astype(F32)[8:16]
            pair = jnp.concatenate([own, own], axis=0)
            table = jnp.where(sub16 == r, pair, table)
            for k in range(4):
                selt[r, pl.ds(8 * k, 8), :] = own * 32.0 + (sub8 + 8 * k).astype(F32)
        sels[0] = table.astype(BF16)
        for o in range(1, 8):
            dy, dc = row[o]
            back = index_of(-dy, dc)
            send(sels.at[0], sels.at[back], es.at[o - 1], er.at[back - 1], dev(dy=dy, dc=dc))
        for p in range(4):
            r = my_home(p)
            t = lax.rem(8 - r, 8)
            down = (lax.broadcasted_iota(jnp.int32, (QR, 128), 1)
                    == t * 8 + (lax.broadcasted_iota(jnp.int32, (QR, 128), 0) >> 5)).astype(F32).astype(BF16)
            across = (lax.broadcasted_iota(jnp.int32, (16, 128), 0)
                      == xh * 4 + (lax.broadcasted_iota(jnp.int32, (16, 128), 1) >> 5)).astype(F32).astype(BF16)
            ask[p] = dot(dot(down, meta[r], 1, 1).astype(BF16), across, 1, 0)

    jl = lax.broadcasted_iota(jnp.int32, (BR, PR), 1).astype(F32)

    def pick(o):
        dy, dc = row[o]
        for r in range(NZ):
            k = ((8 - r) % 8) * 8 + o
            want = jnp.broadcast_to(selt[r, :, k:k + 1], (BR, PR))
            bsel[pl.ds(r * BR, BR), :] = (want == jl).astype(F32).astype(BF16)

        def part(n, _):
            cols = pl.ds(pl.multiple_of(n * 256, 256), 256)
            got = dot(bsel[...], pb[dy, dc, :, cols], 1, 0).astype(BF16)
            for r in range(NZ):
                psel[r, pl.ds(o * BR, BR), cols] = got[r * BR:(r + 1) * BR]
            return 0

        lax.fori_loop(0, 4, part, 0)

    groups = (pl.ds(0, 64), pl.ds(64, 128), pl.ds(192, 64))

    def score(r, g, halves):
        home = lax.rem(z + r, 8)
        p, m = lax.rem(home, 4), home // 4
        part = groups[g]
        first, n = halves[0] * 128, len(halves) * 128
        got = dot(psel[r, part, :], qb[r, pl.ds(first, n), :], 1, 1)
        for half in halves:
            xt = 2 * m + half
            st[p, xt, part, :] = got[:, half * 128 - first:half * 128 - first + 128]
            slot = lax.rem(x - xt + 4, 4) - 1
            send(st.at[p, xt, part], srv.at[p, slot, part], ss.at[r, g, half], sr.at[p, g, slot], (dp, xt), when=xt != x)

    rowi = lax.broadcasted_iota(jnp.int32, (QR, 128), 0)
    lanei = lax.broadcasted_iota(jnp.int32, (QR, 128), 1)
    same_row = (rowi & 31) == (lanei & 31)

    def row_stats():
        scale = jnp.zeros((8, 128), F32)
        hits = jnp.zeros((8, 128), F32)
        for n in (2, 1, 3, 0):
            p = lax.rem(z + n, 4)
            for g in range(3):
                for k in range(3):
                    arrived(srv.at[p, k, groups[g]], sr.at[p, g, k])
            summed = st[p, x] + srv[p, 0] + srv[p, 1] + srv[p, 2]
            live = ask[p] > 0.5
            logits = jnp.where(live, summed * (D ** -0.5), -1e30)
            lg[p] = logits
            top = jnp.max(logits, axis=0, keepdims=True)
            total = jnp.sum(jnp.where(live, jnp.exp(logits - top), 0.0), axis=0, keepdims=True)
            pos = jnp.sum(jnp.where((ask[p] > 1.5) & same_row, logits, 0.0), axis=0, keepdims=True)
            scale = jnp.where(sub8 == p, top, jnp.where(sub8 == 4 + p, total, scale))
            hits = jnp.where(sub8 == p, pos, hits)
        stat[0, 0] = scale
        stat[1, 0] = hits
        for n in range(2):
            for d in range(1, NZ):
                send(stat.at[n, 0], stat.at[n, 8 - d], ts.at[n, d - 1], tr.at[n, 7 - d], dev(dz=d))

    def prepare(r):
        line = lax.broadcasted_iota(jnp.int32, (1, QR), 1)
        want = jnp.zeros((1, QR), F32)
        for j in range(8):
            dy, dc = row[j]
            k = ((8 - r) % 8) * 8 + index_of(-dy, dc)
            asked = jnp.broadcast_to(sels[j].astype(F32)[r:r + 1, k:k + 1], (1, QR))
            want = jnp.where((line >> 5) == j, asked * 32.0 + (line & 31).astype(F32), want)
        down = lax.broadcasted_iota(jnp.int32, (PR, QR), 0).astype(F32)
        bback[r] = (down == want).astype(F32).astype(BF16)

    here, scored = {(0, 0), (0, 1)}, set()

    def slot_events(t):
        k, j = t // 4 + 1, t % 4
        q_arrived(k, j)
        if k < 3 or (k == 3 and j < 2):
            send_q(k, j)
        if k == 4 and j == 1:
            here.update(((4, 0), (4, 1)))
        elif k < 4 and j % 2:
            here.update(((8 - k, j // 2), (k, 1 - j // 2)))
        if t < 12:
            ip, im = p_part(t)
            a, b = (3, 1) if t < 8 else (2, 2)
            arrived(pb.at[a, 0, rows(ip)], pr.at[0, t])
            arrived(pb.at[b, 0, rows(im)], pr.at[1, t])
            if t < 4:
                send_p(t + 8)
            if t == 3:
                send_sib(3, 0, 256, 6)
                send_sib(1, 1, 256, 3)
            if t == 7:
                send_sib(3, 1, 256, 7)
                send_sib(1, 0, 256, 2)
            if t > 7:
                send_sib(2, ip, 64, 8 + ip)
                send_sib(2, im, 64, 8 + im)

    def score_new(g):
        for r in range(8):
            halves = [half for half in range(2) if (r, half) in here and (r, g, half) not in scored]
            if halves:
                score(r, g, halves)
                scored.update((r, g, half) for half in halves)

    for t in range(14):
        slot_events(t)
        if t == 0:
            take_lists()
            load_q.wait()
            load_p.wait()
        if t == 1:
            pick(0)
        if t == 2:
            sib_arrived(0)
            pick(1)
        if t == 9:
            for o in range(1, 8):
                arrived(sels.at[o], er.at[o - 1])
        if 9 <= t < 11:
            prepare(2 * t - 18)
            prepare(2 * t - 17)
        if t == 7:
            pick(2)
            pick(4)
        if t == 8:
            sib_arrived(1)
            pick(3)
            sib_arrived(3)
            pick(5)
        if t >= 2:
            score_new(0)
        if t >= 8:
            score_new(1)
        if t == 11:
            pick(6)
            sib_arrived(2)
            pick(7)
        if t >= 11:
            score_new(2)
    assert len(scored) == 48
    row_stats()
    for r in range(4, 8):
        prepare(r)

    for d in range(1, NZ):
        arrived(stat.at[0, d], tr.at[0, d - 1])
    top = stat[0, 0, 0:4]
    for d in range(1, NZ):
        top = jnp.maximum(top, stat[0, d, 0:4])
    total = jnp.zeros((4, 128), F32)
    for d in range(NZ):
        total = total + stat[0, d, 4:8] * jnp.exp(stat[0, d, 0:4] - top)
    norm[0:4] = top
    norm[4:8] = 1.0 / total

    def weigh(s):
        p = lax.rem(z + s, 4)
        r = my_home(p)
        hot = jnp.where((ask[p] > 1.5) & same_row, 1.0, 0.0)
        wt[r, xh] = (jnp.exp(lg[p] - norm[pl.ds(p, 1), :]) * norm[pl.ds(4 + p, 1), :] - hot).astype(BF16)
        for d in range(1, NX):
            send(wt.at[r, xh], wt.at[r, xh], ws.at[s, d - 1], wr.at[r, xh], dev(dx=d))

    for s in (0, 3, 1, 2):
        weigh(s)
    for d in range(1, NZ):
        arrived(stat.at[1, d], tr.at[1, d - 1])
    pos = jnp.zeros((4, 128), F32)
    for d in range(NZ):
        pos = pos + stat[1, d, 0:4]
    losses = (top - pos) + jnp.log(total)
    own_pair = lax.rem(z, 4)
    tile = jnp.zeros((1, 128), F32)
    for p in range(4):
        tile = jnp.where(own_pair == p, losses[p:p + 1], tile)
    lossb[x] = jnp.broadcast_to(tile, (8, 128))
    for d in range(1, NX):
        send(lossb.at[x], lossb.at[x], ls.at[d - 1], lr.at[3 - d], dev(dx=d))

    def weights_arrived(r):
        home = lax.rem(z + r, 8)
        for half in range(2):
            @pl.when(2 * (home // 4) + half != x)
            def _():
                arrived(wt.at[r, half], wr.at[r, half])

    def weights(r):
        return jnp.concatenate([wt[r, 0], wt[r, 1]], axis=1)

    def panels(r):
        def part(n, _):
            cols = pl.ds(pl.multiple_of(n * 256, 256), 256)
            pn[r, :, cols] = dot(weights(r), qb[r, :, cols], 1, 0).astype(BF16)
            return 0

        lax.fori_loop(0, 4, part, 0)
        for o in range(1, 8):
            dy, dc = row[o]
            back = index_of(-dy, dc)
            send(pn.at[r, pl.ds(o * BR, BR)], rb.at[r, pl.ds(back * BR, BR)], ns.at[r, o - 1], nr.at[r, back - 1],
                 dev(dy=dy, dc=dc))
        rb[r, pl.ds(0, BR), :] = pn[r, pl.ds(0, BR), :]

    def grads(r):
        def part(n, _):
            cols = pl.ds(pl.multiple_of(n * 256, 256), 256)
            gf[r, :, cols] = dot(weights(r), psel[r, :, cols], 0, 0)
            return 0

        lax.fori_loop(0, 4, part, 0)

    def pass_on(side, h, i, add):
        mineb, came = (gsp, grp) if side == 0 else (gsm, grm)
        r = 4 - h if side == 0 else (4 + h) % 8
        value = gf[r, rows(i), :]
        if add:
            arrived(came.at[h - 1, rows(i)], gr.at[side, h - 1, i])
            value = value + came[h - 1, rows(i), :].astype(F32)
        mineb[h, rows(i), :] = value.astype(BF16)
        send(mineb.at[h, rows(i)], came.at[h, rows(i)], gs.at[side, h, i], gr.at[side, h, i],
             dev(dz=1 if side == 0 else NZ - 1))

    weights_arrived(4)
    grads(4)
    for k in range(2):
        pass_on(0, 0, k, False)
        pass_on(1, 0, 2 + k, False)
    panels(4)
    weights_arrived(0)
    panels(0)
    for r in (3, 5):
        weights_arrived(r)
        grads(r)
        for k in range(2):
            pass_on(0 if r == 3 else 1, 1, (2 + k) if r == 3 else k, False)
        panels(r)
        weights_arrived((r + 4) % 8)
        panels((r + 4) % 8)
    for k in range(2):
        pass_on(0, 1, k, True)
        pass_on(1, 1, 2 + k, True)
    for r in (2, 6):
        weights_arrived(r)
        grads(r)
        panels(r)
    for h in range(2, 4):
        if h == 3:
            grads(1)
            grads(7)
        for k in range(4):
            pass_on(0, h, (k + 2) % 4, True)
            pass_on(1, h, k, True)
    grads(0)

    def collect(r, first):
        for j in range(1, 8):
            arrived(rb.at[r, pl.ds(j * BR, BR)], nr.at[r, j - 1])

        def part(n, _):
            cols = pl.ds(pl.multiple_of(n * 256, 256), 256)
            term = dot(bback[r], rb[r, :, cols], 1, 0)
            acc[:, cols] = term if first else acc[:, cols] + term
            return 0

        lax.fori_loop(0, 4, part, 0)

    for n, r in enumerate((4, 0, 3, 7, 5, 1, 2)):
        collect(r, n == 0)
    for k in range(4):
        ip, im = (k + 2) % 4, k
        arrived(grp.at[3, rows(ip)], gr.at[0, 3, ip])
        arrived(grm.at[3, rows(im)], gr.at[1, 3, im])
    for k in range(4):
        qg_ref[rows(k), :] = (gf[0, rows(k), :] + grp[3, rows(k), :].astype(F32) + grm[3, rows(k), :].astype(F32)).astype(BF16)
    for d in range(1, NX):
        other = lax.rem(x + d, NX)
        arrived(lossb.at[other], lr.at[d - 1])
    for half in range(2):
        loss_ref[half:half + 1, :] = lossb[2 * (z // 4) + half][0:1]
    collect(6, False)
    for k in range(8):
        pg_ref[rows(k), :] = acc[rows(k), :].astype(BF16)
    for args, when in sent:
        if when is None:
            remote(*args).wait_send()
        else:
            @pl.when(when)
            def _():
                remote(*args).wait_send()


def body(queries, passages, pos_ids, neg_ids, counts):
    dma = pltpu.SemaphoreType.DMA
    vm = pltpu.VMEM
    loss, query_grad, passage_grad = pl.pallas_call(
        kernel,
        out_shape=(jax.ShapeDtypeStruct((2, 128), F32), jax.ShapeDtypeStruct((QR, W), BF16), jax.ShapeDtypeStruct((PR, W), BF16)),
        in_specs=[pl.BlockSpec(memory_space=pltpu.SMEM)] * 3 + [pl.BlockSpec(memory_space=pl.ANY)] * 2,
        out_specs=tuple([pl.BlockSpec(memory_space=pltpu.VMEM)] * 3),
        scratch_shapes=[
            vm((8, QR, W), BF16), vm((NY, NC, PR, W), BF16), vm((8, QR, W), BF16), vm((QR, PR), BF16), vm((8, PR, QR), BF16),
            vm((8, 16, 128), BF16), vm((8, 16, 128), BF16), vm((8, BR, 128), F32), vm((4, QR, 128), F32),
            vm((4, 4, QR, 128), F32), vm((4, 3, QR, 128), F32), vm((4, QR, 128), F32),
            vm((2, 8, 8, 128), F32), vm((8, 128), F32), vm((8, 2, QR, 128), BF16), vm((NX, 8, 128), F32),
            vm((8, QR, W), F32), vm((4, QR, W), BF16), vm((4, QR, W), BF16), vm((4, QR, W), BF16), vm((4, QR, W), BF16),
            vm((8, QR, W), BF16), vm((8, QR, W), BF16), vm((PR, W), F32),
            dma((2,)), dma((2, 14)), dma((2, 14)), dma((2, 12)), dma((2, 12)), dma((16,)), dma((16,)), dma((7,)), dma((7,)),
            dma((7,)), dma((7,)), dma((8, 3, 2)), dma((4, 3, 3)), dma((2, 7)), dma((2, 7)), dma((4, 3)), dma((8, 2)),
            dma((3,)), dma((3,)), dma((2, 4, 4)), dma((2, 4, 4)), dma((8, 7)), dma((8, 7)),
        ],
        compiler_params=pltpu.CompilerParams(collective_id=0, has_side_effects=True, vmem_limit_bytes=60 * 2**20),
        cost_estimate=pl.CostEstimate(flops=10**10, bytes_accessed=4 * 10**6, transcendentals=10**6),
    )(pos_ids, neg_ids, counts, queries, passages)
    return loss.reshape(QR), query_grad, passage_grad


def solution(mesh):
    assert mesh.shape["dp"] == NZ * NY * NC and mesh.shape["mp"] == NX
    return jax.shard_map(
        body,
        mesh=mesh,
        in_specs=(P("dp", "mp"), P("dp", "mp"), P("dp"), P("dp", None), P("dp")),
        out_specs=(P("dp"), P("dp", "mp"), P("dp", "mp")),
        check_vma=False,
    )
```

```python
import jax
import jax.numpy as jnp
from jax import lax
from jax.experimental import pallas as pl
from jax.experimental.pallas import tpu as pltpu
from jax.sharding import PartitionSpec as P

D = 4096
BR = 32
NZ, NY, NC, NX = 8, 4, 2, 4
RY = (0, 1, 3, 2)
W = 1024
QR = 256
PR = 512
MESH = pl.DeviceIdType.MESH
F32 = jnp.float32
BF16 = jnp.bfloat16


def index_of(dy, dc):
    return RY.index(dy % NY) * NC + dc


def dot(a, b, ca, cb):
    return lax.dot_general(a, b, (((ca,), (cb,)), ((), ())), preferred_element_type=F32)


def kernel(pos_ref, neg_ref, cnt_ref, q_hbm, p_hbm, loss_ref, qg_ref, pg_ref,
           qb, pb, psel, bsel, bback, meta, sels, selt, ask, st, srv, lg, stat, norm, wt, lossb,
           gf, gsp, gsm, grp, grm, pn, rb, acc, qrow, wrow,
           lsem, qs, qr, ps, pr, sibs, sibr, ms, mr, es, er, ss, sr, ts, tr, ws, wr, ls, lr, gs, gr, ns, nr, ys, yr, fs, fr, vs, vr):
    dp = lax.axis_index("dp")
    x = lax.axis_index("mp")
    z = dp // (NY * NC)
    y = lax.rem(dp // NC, NY)
    c = lax.rem(dp, NC)
    xm, xh = lax.rem(x, 2), x // 2

    def dev(dz=0, dy=0, dc=0, dx=0):
        there = lax.rem(z + dz, NZ) * (NY * NC) + lax.rem(y + dy, NY) * NC + lax.rem(c + dc, NC)
        return (there, lax.rem(x + dx, NX))

    row = [(RY[o // NC], o % NC) for o in range(8)]
    peers = [dev(dz=d) for d in range(1, NZ)] + [dev(dy=a, dc=b) for a, b in row[1:]] + [dev(dx=d) for d in range(1, NX)]
    barrier = pltpu.get_barrier_semaphore()
    for p in peers:
        pl.semaphore_signal(barrier, 1, device_id=p, device_id_type=MESH)

    load_q = pltpu.make_async_copy(q_hbm, qb.at[0], lsem.at[0])
    load_p = pltpu.make_async_copy(p_hbm, pb.at[0, 0], lsem.at[1])
    load_q.start()
    load_p.start()

    sent = []

    def remote(src, dst, ssem, rsem, to):
        return pltpu.make_async_remote_copy(src_ref=src, dst_ref=dst, send_sem=ssem, recv_sem=rsem, device_id=to, device_id_type=MESH)

    def send(*args, when=None):
        if when is None:
            remote(*args).start()
        else:
            @pl.when(when)
            def _():
                remote(*args).start()
        sent.append((args, when))

    def arrived(dst, rsem):
        remote(dst, dst, rsem, rsem, peers[0]).wait_recv()

    def rows(i, n=64):
        return pl.ds(i * n, n)

    def send_q(k, j):
        i = k * 4 + j
        right, left = (q_hbm, q_hbm) if k == 0 else (qb.at[8 - k], qb.at[k])
        send(right.at[rows(j)], qb.at[7 - k, rows(j)], qs.at[0, i], qr.at[0, i], dev(dz=1))
        jm = (j + 2) % 4
        send(left.at[rows(jm)], qb.at[k + 1, rows(jm)], qs.at[1, i], qr.at[1, i], dev(dz=NZ - 1))

    def q_arrived(k, j):
        i = (k - 1) * 4 + j
        arrived(qb.at[8 - k, rows(j)], qr.at[0, i])
        arrived(qb.at[k, rows((j + 2) % 4)], qr.at[1, i])

    def send_row_q(t):
        up, down = (qb.at[0], qb.at[0]) if t < 4 else (qrow.at[3, 0], qrow.at[1, 0])
        a, b = (3, 1) if t < 4 else (2, 2)
        ip, im = (t, (t + 2) % 4) if t < 4 else (t - 4, t - 2)
        send(up.at[rows(ip)], qrow.at[a, 0, rows(ip)], ys.at[0, t], yr.at[0, t], dev(dy=1))
        send(down.at[rows(im)], qrow.at[b, 0, rows(im)], ys.at[1, t], yr.at[1, t], dev(dy=NY - 1))

    def row_q_arrived(t):
        a, b = (3, 1) if t < 4 else (2, 2)
        ip, im = (t, (t + 2) % 4) if t < 4 else (t - 4, t - 2)
        arrived(qrow.at[a, 0, rows(ip)], yr.at[0, t])
        arrived(qrow.at[b, 0, rows(im)], yr.at[1, t])

    def send_row_sib(a):
        send(qb.at[0] if a == 0 else qrow.at[a, 0], qrow.at[a, 1], fs.at[a], fr.at[a], dev(dc=1))

    def p_part(t):
        if t < 8:
            return t, (t + 4) % 8
        return t - 8, t - 4

    def send_p(t):
        ip, im = p_part(t)
        up, down = (p_hbm, p_hbm) if t < 8 else (pb.at[3, 0], pb.at[1, 0])
        a, b = (3, 1) if t < 8 else (2, 2)
        send(up.at[rows(ip)], pb.at[a, 0, rows(ip)], ps.at[0, t], pr.at[0, t], dev(dy=1))
        send(down.at[rows(im)], pb.at[b, 0, rows(im)], ps.at[1, t], pr.at[1, t], dev(dy=NY - 1))

    def send_sib(a, i, n, k):
        send((p_hbm if a == 0 else pb.at[a, 0]).at[rows(i, n)], pb.at[a, 1, rows(i, n)], sibs.at[k], sibr.at[k], dev(dc=1))

    def sib_arrived(a):
        if a == 2:
            for i in range(8):
                arrived(pb.at[2, 1, rows(i)], sibr.at[8 + i])
        else:
            for half in range(2):
                arrived(pb.at[a, 1, rows(half, 256)], sibr.at[2 * a + half])

    lane = lax.broadcasted_iota(jnp.int32, (8, 128), 1)
    sub8 = lax.broadcasted_iota(jnp.int32, (8, 128), 0)
    o_l = lane & 7
    og = o_l >> 1
    ry_l = og ^ (og >> 1)
    owner = (((z + (lane >> 3)) & 7) << 3) + (((y + ry_l) & 3) << 1) + (c ^ (o_l & 1))
    owner = jnp.where(lane < 64, owner, -7)
    code = jnp.zeros((8, 128), jnp.int32)
    sel = jnp.full((8, 128), -1, jnp.int32)
    for s in range(8):
        col = jnp.full((8, 128), -1, jnp.int32)
        for b in range(8):
            block = pos_ref[b] if s == 0 else jnp.where(s - 1 < cnt_ref[b], neg_ref[b, s - 1], -1)
            col = jnp.where(sub8 == b, block, col)
        hit = (col >= 0) & ((col >> 4) == owner)
        code = jnp.where(hit, 2 if s == 0 else 1, code)
        sel = jnp.where(hit, col & 15, sel)
    sel = jnp.broadcast_to(jnp.max(sel, axis=0, keepdims=True), (8, 128))
    meta[0] = jnp.concatenate([code, sel], axis=0).astype(F32).astype(BF16)
    pl.semaphore_wait(barrier, len(peers))
    for d in range(1, NZ):
        send(meta.at[0], meta.at[8 - d], ms.at[d - 1], mr.at[7 - d], dev(dz=d))
    for j in range(4):
        send_q(0, j)
        send_p(j)
    for t in range(4, 8):
        send_p(t)
    send_sib(0, 0, 256, 0)
    send_sib(0, 1, 256, 1)

    def my_home(p):
        return lax.rem(p + 4 * xm - z + 8, 8)

    def take_lists():
        for r in range(1, NZ):
            arrived(meta.at[r], mr.at[r - 1])
        sub16 = lax.broadcasted_iota(jnp.int32, (16, 128), 0)
        table = jnp.zeros((16, 128), F32)
        for r in range(NZ):
            own = meta[r].astype(F32)[8:16]
            pair = jnp.concatenate([own, own], axis=0)
            table = jnp.where(sub16 == r, pair, table)
            for k in range(4):
                selt[r, pl.ds(8 * k, 8), :] = own * 32.0 + (sub8 + 8 * k).astype(F32)
        sels[0] = table.astype(BF16)
        for o in range(1, 8):
            dy, dc = row[o]
            back = index_of(-dy, dc)
            send(sels.at[0], sels.at[back], es.at[o - 1], er.at[back - 1], dev(dy=dy, dc=dc))
        for p in range(4):
            r = my_home(p)
            t = lax.rem(8 - r, 8)
            down = (lax.broadcasted_iota(jnp.int32, (QR, 128), 1)
                    == t * 8 + (lax.broadcasted_iota(jnp.int32, (QR, 128), 0) >> 5)).astype(F32).astype(BF16)
            across = (lax.broadcasted_iota(jnp.int32, (16, 128), 0)
                      == xh * 4 + (lax.broadcasted_iota(jnp.int32, (16, 128), 1) >> 5)).astype(F32).astype(BF16)
            ask[p] = dot(dot(down, meta[r], 1, 1).astype(BF16), across, 1, 0)

    jl = lax.broadcasted_iota(jnp.int32, (BR, PR), 1).astype(F32)

    def pick(o):
        dy, dc = row[o]
        for r in range(NZ):
            k = ((8 - r) % 8) * 8 + o
            want = jnp.broadcast_to(selt[r, :, k:k + 1], (BR, PR))
            bsel[pl.ds(r * BR, BR), :] = (want == jl).astype(F32).astype(BF16)

        def part(n, _):
            cols = pl.ds(pl.multiple_of(n * 256, 256), 256)
            got = dot(bsel[...], pb[dy, dc, :, cols], 1, 0).astype(BF16)
            for r in range(NZ):
                psel[r, pl.ds(o * BR, BR), cols] = got[r * BR:(r + 1) * BR]
            return 0

        lax.fori_loop(0, 4, part, 0)

    bounds = (0, 64, 192, 256)

    def score(r, gs_, halves):
        home = lax.rem(z + r, 8)
        p, m = lax.rem(home, 4), home // 4
        part = pl.ds(bounds[gs_[0]], bounds[gs_[-1] + 1] - bounds[gs_[0]])
        first, n = halves[0] * 128, len(halves) * 128
        got = dot(psel[r, part, :], qb[r, pl.ds(first, n), :], 1, 1)
        for half in halves:
            xt = m + 2 * half
            st[p, xt, part, :] = got[:, half * 128 - first:half * 128 - first + 128]
            slot = lax.rem(x - xt + 4, 4) - 1
            send(st.at[p, xt, part], srv.at[p, slot, part], ss.at[r, gs_[0], half], sr.at[p, slot], (dp, xt), when=xt != x)

    rowi = lax.broadcasted_iota(jnp.int32, (QR, 128), 0)
    lanei = lax.broadcasted_iota(jnp.int32, (QR, 128), 1)
    same_row = (rowi & 31) == (lanei & 31)

    def send_stats(n):
        for d in range(1, NZ):
            send(stat.at[n, 0], stat.at[n, 8 - d], ts.at[n, d - 1], tr.at[n, 7 - d], dev(dz=d))

    def row_stats():
        scale = jnp.zeros((8, 128), F32)
        hits = jnp.zeros((8, 128), F32)
        for n in (2, 1, 3, 0):
            p = lax.rem(z + n, 4)
            for k in range(3):
                arrived(srv.at[p, k], sr.at[p, k])
            summed = st[p, x] + srv[p, 0] + srv[p, 1] + srv[p, 2]
            live = ask[p] > 0.5
            logits = jnp.where(live, summed * (D ** -0.5), -1e30)
            lg[p] = logits
            top = jnp.max(logits, axis=0, keepdims=True)
            total = jnp.sum(jnp.where(live, jnp.exp(logits - top), 0.0), axis=0, keepdims=True)
            pos = jnp.sum(jnp.where((ask[p] > 1.5) & same_row, logits, 0.0), axis=0, keepdims=True)
            scale = jnp.where(sub8 == p, top, jnp.where(sub8 == 4 + p, total, scale))
            hits = jnp.where(sub8 == p, pos, hits)
        stat[0, 0] = scale
        stat[1, 0] = hits
        send_stats(0)

    def prepare(r):
        line = lax.broadcasted_iota(jnp.int32, (1, QR), 1)
        want = jnp.zeros((1, QR), F32)
        for j in range(8):
            dy, dc = row[j]
            k = ((8 - r) % 8) * 8 + index_of(-dy, dc)
            asked = jnp.broadcast_to(sels[j].astype(F32)[r:r + 1, k:k + 1], (1, QR))
            want = jnp.where((line >> 5) == j, asked * 32.0 + (line & 31).astype(F32), want)
        down = lax.broadcasted_iota(jnp.int32, (PR, QR), 0).astype(F32)
        bback[r] = (down == want).astype(F32).astype(BF16)

    here, scored = {(0, 0), (0, 1)}, set()

    def slot_events(t):
        k, j = t // 4 + 1, t % 4
        q_arrived(k, j)
        if k < 3 or (k == 3 and j < 2):
            send_q(k, j)
        if k == 4 and j == 1:
            here.update(((4, 0), (4, 1)))
        elif k < 4 and j % 2:
            here.update(((8 - k, j // 2), (k, 1 - j // 2)))
        if t < 12:
            ip, im = p_part(t)
            a, b = (3, 1) if t < 8 else (2, 2)
            arrived(pb.at[a, 0, rows(ip)], pr.at[0, t])
            arrived(pb.at[b, 0, rows(im)], pr.at[1, t])
            if t < 4:
                send_p(t + 8)
            if t == 3:
                send_sib(3, 0, 256, 6)
                send_sib(1, 1, 256, 3)
            if t == 7:
                send_sib(3, 1, 256, 7)
                send_sib(1, 0, 256, 2)
            if t > 7:
                send_sib(2, ip, 64, 8 + ip)
                send_sib(2, im, 64, 8 + im)

    def score_new(upto):
        for r in (1, 5, 2, 6, 3, 7, 0, 4):
            todo = {}
            for half in range(2):
                left = tuple(g for g in range(upto + 1) if (r, half) in here and (r, g, half) not in scored)
                if left:
                    todo.setdefault(left, []).append(half)
            for left, halves in todo.items():
                score(r, left, halves)
                scored.update((r, g, half) for g in left for half in halves)

    for t in range(14):
        slot_events(t)
        if t == 0:
            take_lists()
            load_q.wait()
            load_p.wait()
        if t == 1:
            pick(0)
        if t == 2:
            sib_arrived(0)
            pick(1)
        if t == 9:
            for o in range(1, 8):
                arrived(sels.at[o], er.at[o - 1])
        if 9 <= t < 11:
            prepare(2 * t - 18)
            prepare(2 * t - 17)
        if t == 7:
            pick(2)
            pick(4)
            sib_arrived(1)
            pick(3)
            sib_arrived(3)
            pick(5)
        if 2 <= t < 7:
            score_new(0)
        if 7 <= t < 12:
            score_new(1)
        if t == 11:
            pick(6)
            sib_arrived(2)
            pick(7)
            for n in range(4):
                send_row_q(n)
            send_row_sib(0)
        if t >= 11:
            score_new(2)
    for n in range(2):
        row_q_arrived(n)
        send_row_q(n + 4)
    assert len(scored) == 48
    row_stats()
    for r in range(4, 8):
        prepare(r)
    row_q_arrived(2)
    row_q_arrived(3)
    send_row_sib(1)
    send_row_sib(3)

    for d in range(1, NZ):
        arrived(stat.at[0, d], tr.at[0, d - 1])
    top = stat[0, 0, 0:4]
    for d in range(1, NZ):
        top = jnp.maximum(top, stat[0, d, 0:4])
    total = jnp.zeros((4, 128), F32)
    for d in range(NZ):
        total = total + stat[0, d, 4:8] * jnp.exp(stat[0, d, 0:4] - top)
    norm[0:4] = top
    norm[4:8] = 1.0 / total

    def weigh(s):
        p = lax.rem(z + s, 4)
        r = my_home(p)
        hot = jnp.where((ask[p] > 1.5) & same_row, 1.0, 0.0)
        wt[r, xh] = (jnp.exp(lg[p] - norm[pl.ds(p, 1), :]) * norm[pl.ds(4 + p, 1), :] - hot).astype(BF16)
        for d in range(1, NX):
            send(wt.at[r, xh], wt.at[r, xh], ws.at[s, d - 1], wr.at[r, xh], dev(dx=d))

    for s in (0, 3, 1, 2):
        weigh(s)
    send_stats(1)
    row_q_arrived(4)
    row_q_arrived(5)
    send_row_sib(2)
    for d in range(1, NZ):
        arrived(stat.at[1, d], tr.at[1, d - 1])
    pos = jnp.zeros((4, 128), F32)
    for d in range(NZ):
        pos = pos + stat[1, d, 0:4]
    losses = (top - pos) + jnp.log(total)
    own_pair = lax.rem(z, 4)
    tile = jnp.zeros((1, 128), F32)
    for p in range(4):
        tile = jnp.where(own_pair == p, losses[p:p + 1], tile)
    lossb[x] = jnp.broadcast_to(tile, (8, 128))
    for d in range(1, NX):
        send(lossb.at[x], lossb.at[x], ls.at[d - 1], lr.at[3 - d], dev(dx=d))

    def weights_arrived(r):
        home = lax.rem(z + r, 8)
        for half in range(2):
            @pl.when(home // 4 + 2 * half != x)
            def _():
                arrived(wt.at[r, half], wr.at[r, half])

    def weights(r):
        return jnp.concatenate([wt[r, 0], wt[r, 1]], axis=1)

    def panels(r):
        def part(n, _):
            cols = pl.ds(pl.multiple_of(n * 256, 256), 256)
            pn[r, :, cols] = dot(weights(r), qb[r, :, cols], 1, 0).astype(BF16)
            return 0

        lax.fori_loop(0, 4, part, 0)
        for o in range(1, 8):
            dy, dc = row[o]
            back = index_of(-dy, dc)
            send(pn.at[r, pl.ds(o * BR, BR)], rb.at[r, pl.ds(back * BR, BR)], ns.at[r, o - 1], nr.at[r, back - 1],
                 dev(dy=dy, dc=dc))
        rb[r, pl.ds(0, BR), :] = pn[r, pl.ds(0, BR), :]

    def grads(r):
        def part(n, _):
            cols = pl.ds(pl.multiple_of(n * 256, 256), 256)
            gf[r, :, cols] = dot(weights(r), psel[r, :, cols], 0, 0)
            return 0

        lax.fori_loop(0, 4, part, 0)

    def pass_on(side, h, i, add):
        mineb, came = (gsp, grp) if side == 0 else (gsm, grm)
        r = 4 - h if side == 0 else (4 + h) % 8
        value = gf[r, rows(i), :]
        if add:
            arrived(came.at[h - 1, rows(i)], gr.at[side, h - 1, i])
            value = value + came[h - 1, rows(i), :].astype(F32)
        mineb[h, rows(i), :] = value.astype(BF16)
        send(mineb.at[h, rows(i)], came.at[h, rows(i)], gs.at[side, h, i], gr.at[side, h, i],
             dev(dz=1 if side == 0 else NZ - 1))

    weights_arrived(4)
    grads(4)
    for k in range(2):
        pass_on(0, 0, k, False)
        pass_on(1, 0, 2 + k, False)
    panels(4)
    weights_arrived(0)
    for o in range(1, 8):
        dy, dc = row[o]
        back = index_of(-dy, dc)
        for half in range(2):
            send(wt.at[0, half, pl.ds(o * BR, BR)], wrow.at[back, half], vs.at[o - 1, half], vr.at[back - 1, half], dev(dy=dy, dc=dc))
    for r in (3, 5):
        weights_arrived(r)
        grads(r)
        for k in range(2):
            pass_on(0 if r == 3 else 1, 1, (2 + k) if r == 3 else k, False)
        panels(r)
        weights_arrived((r + 4) % 8)
        panels((r + 4) % 8)
    for k in range(2):
        pass_on(0, 1, k, True)
        pass_on(1, 1, 2 + k, True)
    for r in (2, 6):
        weights_arrived(r)
        grads(r)
        panels(r)
    for h in range(2, 4):
        if h == 3:
            grads(1)
            grads(7)
        for k in range(4):
            pass_on(0, h, (k + 2) % 4, True)
            pass_on(1, h, k, True)
    grads(0)

    def row_panels():
        for a in range(NY):
            arrived(qrow.at[a, 1], fr.at[a])
        for j in range(8):
            dy, dc = row[j]
            if j:
                for half in range(2):
                    arrived(wrow.at[j, half], vr.at[j - 1, half])
            w = [wrow[j, half] if j else wt[0, half, 0:BR, :] for half in range(2)]
            w = jnp.concatenate(w, axis=1)
            q = qrow.at[dy, dc] if j else qb.at[0]
            rb[0, pl.ds(j * BR, BR), :] = dot(w, q[...], 1, 0).astype(BF16)

    def collect(r, first=False, last=False):
        if r:
            for j in range(1, 8):
                arrived(rb.at[r, pl.ds(j * BR, BR)], nr.at[r, j - 1])
        else:
            row_panels()

        for n in range(4):
            cols = pl.ds(n * 256, 256)
            term = dot(bback[r], rb[r, :, cols], 1, 0)
            term = term if first else acc[:, cols] + term
            if last:
                pg_ref[:, cols] = term.astype(BF16)
            else:
                acc[:, cols] = term

    for n, r in enumerate((4, 0, 3, 7, 5, 1, 2)):
        collect(r, first=n == 0)
    for k in range(4):
        ip, im = (k + 2) % 4, k
        arrived(grp.at[3, rows(ip)], gr.at[0, 3, ip])
        arrived(grm.at[3, rows(im)], gr.at[1, 3, im])
    for k in range(4):
        qg_ref[rows(k), :] = (gf[0, rows(k), :] + grp[3, rows(k), :].astype(F32) + grm[3, rows(k), :].astype(F32)).astype(BF16)
    for d in range(1, NX):
        other = lax.rem(x + d, NX)
        arrived(lossb.at[other], lr.at[d - 1])
    for half in range(2):
        loss_ref[half:half + 1, :] = lossb[z // 4 + 2 * half][0:1]
    for args, when in sent:
        if when is None:
            remote(*args).wait_send()
        else:
            @pl.when(when)
            def _():
                remote(*args).wait_send()
    collect(6, last=True)


def body(queries, passages, pos_ids, neg_ids, counts):
    dma = pltpu.SemaphoreType.DMA
    vm = pltpu.VMEM
    loss, query_grad, passage_grad = pl.pallas_call(
        kernel,
        out_shape=(pltpu.VMEM((2, 128), F32), pltpu.VMEM((QR, W), BF16), pltpu.VMEM((PR, W), BF16)),
        in_specs=[pl.BlockSpec(memory_space=pltpu.SMEM)] * 3 + [pl.BlockSpec(memory_space=pl.ANY)] * 2,
        out_specs=tuple([pl.BlockSpec(memory_space=pltpu.VMEM)] * 3),
        scratch_shapes=[
            vm((8, QR, W), BF16), vm((NY, NC, PR, W), BF16), vm((8, QR, W), BF16), vm((QR, PR), BF16), vm((8, PR, QR), BF16),
            vm((8, 16, 128), BF16), vm((8, 16, 128), BF16), vm((8, BR, 128), F32), vm((4, QR, 128), F32),
            vm((4, 4, QR, 128), F32), vm((4, 3, QR, 128), F32), vm((4, QR, 128), F32),
            vm((2, 8, 8, 128), F32), vm((8, 128), F32), vm((8, 2, QR, 128), BF16), vm((NX, 8, 128), F32),
            vm((8, QR, W), F32), vm((4, QR, W), BF16), vm((4, QR, W), BF16), vm((4, QR, W), BF16), vm((4, QR, W), BF16),
            vm((8, QR, W), BF16), vm((8, QR, W), BF16), vm((PR, W), F32),
            vm((NY, NC, QR, W), BF16), vm((8, 2, BR, 128), BF16),
            dma((2,)), dma((2, 14)), dma((2, 14)), dma((2, 12)), dma((2, 12)), dma((16,)), dma((16,)), dma((7,)), dma((7,)),
            dma((7,)), dma((7,)), dma((8, 3, 2)), dma((4, 3)), dma((2, 7)), dma((2, 7)), dma((4, 3)), dma((8, 2)),
            dma((3,)), dma((3,)), dma((2, 4, 4)), dma((2, 4, 4)), dma((8, 7)), dma((8, 7)), dma((2, 6)), dma((2, 6)), dma((4,)), dma((4,)),
            dma((7, 2)), dma((7, 2)),
        ],
        compiler_params=pltpu.CompilerParams(collective_id=0, has_side_effects=True, vmem_limit_bytes=60 * 2**20),
        cost_estimate=pl.CostEstimate(flops=10**10, bytes_accessed=4 * 10**6, transcendentals=10**6),
    )(pos_ids, neg_ids, counts, queries, passages)
    return loss.reshape(QR), query_grad, passage_grad


def solution(mesh):
    assert mesh.shape["dp"] == NZ * NY * NC and mesh.shape["mp"] == NX
    return jax.shard_map(
        body,
        mesh=mesh,
        in_specs=(P("dp", "mp"), P("dp", "mp"), P("dp"), P("dp", None), P("dp")),
        out_specs=(P("dp"), P("dp", "mp"), P("dp", "mp")),
        check_vma=False,
    )
```

```python
import jax
import jax.numpy as jnp
from jax import lax
from jax.experimental import pallas as pl
from jax.experimental.pallas import tpu as pltpu
from jax.sharding import PartitionSpec as P

D = 4096
BR = 32
NZ, NY, NC, NX = 8, 4, 2, 4
RY = (0, 1, 3, 2)
W = 1024
QR = 256
PR = 512
MESH = pl.DeviceIdType.MESH
F32 = jnp.float32
BF16 = jnp.bfloat16


def index_of(dy, dc):
    return RY.index(dy % NY) * NC + dc


def dot(a, b, ca, cb):
    return lax.dot_general(a, b, (((ca,), (cb,)), ((), ())), preferred_element_type=F32)


def kernel(pos_hbm, neg_hbm, cnt_hbm, q_hbm, p_hbm, loss_ref, qg_ref, pg_ref,
           qb, pb, psel, bsel, bback, meta, sels, selt, ask, st, srv, lg, stat, norm, wt, lossb,
           gf, gsp, gsm, grp, grm, pn, rb, acc, qrow, wrow, pos_ref, neg_ref, cnt_ref,
           lsem, qs, qr, ps, pr, sibs, sibr, ms, mr, es, er, ss, sr, ts, tr, ws, wr, ls, lr, gs, gr, ns, nr, ys, yr, fs, fr, vs, vr):
    dp = lax.axis_index("dp")
    x = lax.axis_index("mp")
    z = dp // (NY * NC)
    y = lax.rem(dp // NC, NY)
    c = lax.rem(dp, NC)
    xm, xh = lax.rem(x, 2), x // 2

    def dev(dz=0, dy=0, dc=0, dx=0):
        there = lax.rem(z + dz, NZ) * (NY * NC) + lax.rem(y + dy, NY) * NC + lax.rem(c + dc, NC)
        return (there, lax.rem(x + dx, NX))

    row = [(RY[o // NC], o % NC) for o in range(8)]
    peers = [dev(dz=d) for d in range(1, NZ)] + [dev(dy=a, dc=b) for a, b in row[1:]] + [dev(dx=d) for d in range(1, NX)]
    barrier = pltpu.get_barrier_semaphore()
    for p in peers:
        pl.semaphore_signal(barrier, 1, device_id=p, device_id_type=MESH)

    lists = [pltpu.make_async_copy(a, b, lsem.at[2 + n]) for n, (a, b) in enumerate(((pos_hbm, pos_ref), (neg_hbm, neg_ref), (cnt_hbm, cnt_ref)))]
    for one in lists:
        one.start()
    load_q = pltpu.make_async_copy(q_hbm, qb.at[0], lsem.at[0])
    load_p = pltpu.make_async_copy(p_hbm, pb.at[0, 0], lsem.at[1])
    load_q.start()
    load_p.start()

    sent = []

    def remote(src, dst, ssem, rsem, to):
        return pltpu.make_async_remote_copy(src_ref=src, dst_ref=dst, send_sem=ssem, recv_sem=rsem, device_id=to, device_id_type=MESH)

    def send(*args, when=None):
        if when is None:
            remote(*args).start()
        else:
            @pl.when(when)
            def _():
                remote(*args).start()
        sent.append((args, when))

    def arrived(dst, rsem):
        remote(dst, dst, rsem, rsem, peers[0]).wait_recv()

    def rows(i, n=64):
        return pl.ds(i * n, n)

    def send_q(k, j):
        i = k * 4 + j
        right, left = (q_hbm, q_hbm) if k == 0 else (qb.at[8 - k], qb.at[k])
        send(right.at[rows(j)], qb.at[7 - k, rows(j)], qs.at[0, i], qr.at[0, i], dev(dz=1))
        jm = (j + 2) % 4
        send(left.at[rows(jm)], qb.at[k + 1, rows(jm)], qs.at[1, i], qr.at[1, i], dev(dz=NZ - 1))

    def q_arrived(k, j):
        i = (k - 1) * 4 + j
        arrived(qb.at[8 - k, rows(j)], qr.at[0, i])
        arrived(qb.at[k, rows((j + 2) % 4)], qr.at[1, i])

    def send_row_q(t):
        up, down = (qb.at[0], qb.at[0]) if t < 4 else (qrow.at[3, 0], qrow.at[1, 0])
        a, b = (3, 1) if t < 4 else (2, 2)
        ip, im = (t, (t + 2) % 4) if t < 4 else (t - 4, t - 2)
        send(up.at[rows(ip)], qrow.at[a, 0, rows(ip)], ys.at[0, t], yr.at[0, t], dev(dy=1))
        send(down.at[rows(im)], qrow.at[b, 0, rows(im)], ys.at[1, t], yr.at[1, t], dev(dy=NY - 1))

    def row_q_arrived(t):
        a, b = (3, 1) if t < 4 else (2, 2)
        ip, im = (t, (t + 2) % 4) if t < 4 else (t - 4, t - 2)
        arrived(qrow.at[a, 0, rows(ip)], yr.at[0, t])
        arrived(qrow.at[b, 0, rows(im)], yr.at[1, t])

    def send_row_sib(a):
        send(qb.at[0] if a == 0 else qrow.at[a, 0], qrow.at[a, 1], fs.at[a], fr.at[a], dev(dc=1))

    def p_part(t):
        if t < 8:
            return t, (t + 4) % 8
        return t - 8, t - 4

    def send_p(t):
        ip, im = p_part(t)
        up, down = (p_hbm, p_hbm) if t < 8 else (pb.at[3, 0], pb.at[1, 0])
        a, b = (3, 1) if t < 8 else (2, 2)
        send(up.at[rows(ip)], pb.at[a, 0, rows(ip)], ps.at[0, t], pr.at[0, t], dev(dy=1))
        send(down.at[rows(im)], pb.at[b, 0, rows(im)], ps.at[1, t], pr.at[1, t], dev(dy=NY - 1))

    def send_sib(a, i, n, k):
        send((p_hbm if a == 0 else pb.at[a, 0]).at[rows(i, n)], pb.at[a, 1, rows(i, n)], sibs.at[k], sibr.at[k], dev(dc=1))

    def sib_arrived(a):
        if a == 2:
            for i in range(8):
                arrived(pb.at[2, 1, rows(i)], sibr.at[8 + i])
        else:
            for half in range(2):
                arrived(pb.at[a, 1, rows(half, 256)], sibr.at[2 * a + half])

    for one in lists:
        one.wait()
    lane = lax.broadcasted_iota(jnp.int32, (8, 128), 1)
    sub8 = lax.broadcasted_iota(jnp.int32, (8, 128), 0)
    o_l = lane & 7
    og = o_l >> 1
    ry_l = og ^ (og >> 1)
    owner = (((z + (lane >> 3)) & 7) << 3) + (((y + ry_l) & 3) << 1) + (c ^ (o_l & 1))
    owner = jnp.where(lane < 64, owner, -7)
    code = jnp.zeros((8, 128), jnp.int32)
    sel = jnp.full((8, 128), -1, jnp.int32)
    for s in range(8):
        col = jnp.full((8, 128), -1, jnp.int32)
        for b in range(8):
            block = pos_ref[b] if s == 0 else jnp.where(s - 1 < cnt_ref[b], neg_ref[b, s - 1], -1)
            col = jnp.where(sub8 == b, block, col)
        hit = (col >= 0) & ((col >> 4) == owner)
        code = jnp.where(hit, 2 if s == 0 else 1, code)
        sel = jnp.where(hit, col & 15, sel)
    sel = jnp.broadcast_to(jnp.max(sel, axis=0, keepdims=True), (8, 128))
    meta[0] = jnp.concatenate([code, sel], axis=0).astype(F32).astype(BF16)
    pl.semaphore_wait(barrier, len(peers))
    for d in range(1, NZ):
        send(meta.at[0], meta.at[8 - d], ms.at[d - 1], mr.at[7 - d], dev(dz=d))
    for j in range(4):
        send_q(0, j)
        send_p(j)
    for t in range(4, 8):
        send_p(t)
    send_sib(0, 0, 256, 0)
    send_sib(0, 1, 256, 1)

    def my_home(p):
        return lax.rem(p + 4 * xm - z + 8, 8)

    def take_lists():
        for r in range(1, NZ):
            arrived(meta.at[r], mr.at[r - 1])
        sub16 = lax.broadcasted_iota(jnp.int32, (16, 128), 0)
        table = jnp.zeros((16, 128), F32)
        for r in range(NZ):
            own = meta[r].astype(F32)[8:16]
            pair = jnp.concatenate([own, own], axis=0)
            table = jnp.where(sub16 == r, pair, table)
            for k in range(4):
                selt[r, pl.ds(8 * k, 8), :] = own * 32.0 + (sub8 + 8 * k).astype(F32)
        sels[0] = table.astype(BF16)
        for o in range(1, 8):
            dy, dc = row[o]
            back = index_of(-dy, dc)
            send(sels.at[0], sels.at[back], es.at[o - 1], er.at[back - 1], dev(dy=dy, dc=dc))
        for p in range(4):
            r = my_home(p)
            t = lax.rem(8 - r, 8)
            down = (lax.broadcasted_iota(jnp.int32, (QR, 128), 1)
                    == t * 8 + (lax.broadcasted_iota(jnp.int32, (QR, 128), 0) >> 5)).astype(F32).astype(BF16)
            across = (lax.broadcasted_iota(jnp.int32, (16, 128), 0)
                      == xh * 4 + (lax.broadcasted_iota(jnp.int32, (16, 128), 1) >> 5)).astype(F32).astype(BF16)
            ask[p] = dot(dot(down, meta[r], 1, 1).astype(BF16), across, 1, 0)

    jl = lax.broadcasted_iota(jnp.int32, (BR, PR), 1).astype(F32)

    def pick(o):
        dy, dc = row[o]
        for r in range(NZ):
            k = ((8 - r) % 8) * 8 + o
            want = jnp.broadcast_to(selt[r, :, k:k + 1], (BR, PR))
            bsel[pl.ds(r * BR, BR), :] = (want == jl).astype(F32).astype(BF16)

        def part(n, _):
            cols = pl.ds(pl.multiple_of(n * 256, 256), 256)
            got = dot(bsel[...], pb[dy, dc, :, cols], 1, 0).astype(BF16)
            for r in range(NZ):
                psel[r, pl.ds(o * BR, BR), cols] = got[r * BR:(r + 1) * BR]
            return 0

        lax.fori_loop(0, 4, part, 0)

    bounds = (0, 64, 192, 256)

    def score(r, gs_, halves):
        home = lax.rem(z + r, 8)
        p, m = lax.rem(home, 4), home // 4
        part = pl.ds(bounds[gs_[0]], bounds[gs_[-1] + 1] - bounds[gs_[0]])
        first, n = halves[0] * 128, len(halves) * 128
        got = dot(psel[r, part, :], qb[r, pl.ds(first, n), :], 1, 1)
        for half in halves:
            xt = m + 2 * half
            st[p, xt, part, :] = got[:, half * 128 - first:half * 128 - first + 128]
            slot = lax.rem(x - xt + 4, 4) - 1
            send(st.at[p, xt, part], srv.at[p, slot, part], ss.at[r, gs_[0], half], sr.at[p, slot], (dp, xt), when=xt != x)

    rowi = lax.broadcasted_iota(jnp.int32, (QR, 128), 0)
    lanei = lax.broadcasted_iota(jnp.int32, (QR, 128), 1)
    same_row = (rowi & 31) == (lanei & 31)

    def send_stats(n):
        for d in range(1, NZ):
            send(stat.at[n, 0], stat.at[n, 8 - d], ts.at[n, d - 1], tr.at[n, 7 - d], dev(dz=d))

    def row_stats():
        scale = jnp.zeros((8, 128), F32)
        hits = jnp.zeros((8, 128), F32)
        for n in (2, 1, 3, 0):
            p = lax.rem(z + n, 4)
            for k in range(3):
                arrived(srv.at[p, k], sr.at[p, k])
            summed = st[p, x] + srv[p, 0] + srv[p, 1] + srv[p, 2]
            live = ask[p] > 0.5
            logits = jnp.where(live, summed * (D ** -0.5), -1e30)
            lg[p] = logits
            top = jnp.max(logits, axis=0, keepdims=True)
            total = jnp.sum(jnp.where(live, jnp.exp(logits - top), 0.0), axis=0, keepdims=True)
            pos = jnp.sum(jnp.where((ask[p] > 1.5) & same_row, logits, 0.0), axis=0, keepdims=True)
            scale = jnp.where(sub8 == p, top, jnp.where(sub8 == 4 + p, total, scale))
            hits = jnp.where(sub8 == p, pos, hits)
        stat[0, 0] = scale
        stat[1, 0] = hits
        send_stats(0)

    def prepare(r):
        line = lax.broadcasted_iota(jnp.int32, (1, QR), 1)
        want = jnp.zeros((1, QR), F32)
        for j in range(8):
            dy, dc = row[j]
            k = ((8 - r) % 8) * 8 + index_of(-dy, dc)
            asked = jnp.broadcast_to(sels[j].astype(F32)[r:r + 1, k:k + 1], (1, QR))
            want = jnp.where((line >> 5) == j, asked * 32.0 + (line & 31).astype(F32), want)
        down = lax.broadcasted_iota(jnp.int32, (PR, QR), 0).astype(F32)
        bback[r] = (down == want).astype(F32).astype(BF16)

    here, scored = {(0, 0), (0, 1)}, set()

    def slot_events(t):
        k, j = t // 4 + 1, t % 4
        q_arrived(k, j)
        if k < 3 or (k == 3 and j < 2):
            send_q(k, j)
        if k == 4 and j == 1:
            here.update(((4, 0), (4, 1)))
        elif k < 4 and j % 2:
            here.update(((8 - k, j // 2), (k, 1 - j // 2)))
        if t < 12:
            ip, im = p_part(t)
            a, b = (3, 1) if t < 8 else (2, 2)
            arrived(pb.at[a, 0, rows(ip)], pr.at[0, t])
            arrived(pb.at[b, 0, rows(im)], pr.at[1, t])
            if t < 4:
                send_p(t + 8)
            if t == 3:
                send_sib(3, 0, 256, 6)
                send_sib(1, 1, 256, 3)
            if t == 7:
                send_sib(3, 1, 256, 7)
                send_sib(1, 0, 256, 2)
            if t > 7:
                send_sib(2, ip, 64, 8 + ip)
                send_sib(2, im, 64, 8 + im)

    def score_new(upto):
        for r in (1, 5, 2, 6, 3, 7, 0, 4):
            todo = {}
            for half in range(2):
                left = tuple(g for g in range(upto + 1) if (r, half) in here and (r, g, half) not in scored)
                if left:
                    todo.setdefault(left, []).append(half)
            for left, halves in todo.items():
                score(r, left, halves)
                scored.update((r, g, half) for g in left for half in halves)

    for t in range(14):
        slot_events(t)
        if t == 0:
            take_lists()
            load_q.wait()
            load_p.wait()
        if t == 1:
            pick(0)
        if t == 2:
            sib_arrived(0)
            pick(1)
        if t == 9:
            for o in range(1, 8):
                arrived(sels.at[o], er.at[o - 1])
        if 9 <= t < 11:
            prepare(2 * t - 18)
            prepare(2 * t - 17)
        if t == 7:
            pick(2)
            pick(4)
            sib_arrived(1)
            pick(3)
            sib_arrived(3)
            pick(5)
        if 2 <= t < 7:
            score_new(0)
        if 7 <= t < 12:
            score_new(1)
        if t == 11:
            pick(6)
            sib_arrived(2)
            pick(7)
            for n in range(4):
                send_row_q(n)
            send_row_sib(0)
        if t >= 11:
            score_new(2)
    for n in range(2):
        row_q_arrived(n)
        send_row_q(n + 4)
    assert len(scored) == 48
    row_stats()
    for r in range(4, 8):
        prepare(r)
    row_q_arrived(2)
    row_q_arrived(3)
    send_row_sib(1)
    send_row_sib(3)

    for d in range(1, NZ):
        arrived(stat.at[0, d], tr.at[0, d - 1])
    top = stat[0, 0, 0:4]
    for d in range(1, NZ):
        top = jnp.maximum(top, stat[0, d, 0:4])
    total = jnp.zeros((4, 128), F32)
    for d in range(NZ):
        total = total + stat[0, d, 4:8] * jnp.exp(stat[0, d, 0:4] - top)
    norm[0:4] = top
    norm[4:8] = 1.0 / total

    def weigh(s):
        p = lax.rem(z + s, 4)
        r = my_home(p)
        hot = jnp.where((ask[p] > 1.5) & same_row, 1.0, 0.0)
        wt[r, xh] = (jnp.exp(lg[p] - norm[pl.ds(p, 1), :]) * norm[pl.ds(4 + p, 1), :] - hot).astype(BF16)
        for d in range(1, NX):
            send(wt.at[r, xh], wt.at[r, xh], ws.at[s, d - 1], wr.at[r, xh], dev(dx=d))

    weigh(0)
    weigh(3)
    def weights_arrived(r):
        home = lax.rem(z + r, 8)
        for half in range(2):
            @pl.when(home // 4 + 2 * half != x)
            def _():
                arrived(wt.at[r, half], wr.at[r, half])

    def weights(r):
        return jnp.concatenate([wt[r, 0], wt[r, 1]], axis=1)

    def panels(r):
        def part(n, _):
            cols = pl.ds(pl.multiple_of(n * 256, 256), 256)
            pn[r, :, cols] = dot(weights(r), qb[r, :, cols], 1, 0).astype(BF16)
            return 0

        lax.fori_loop(0, 4, part, 0)
        for o in range(1, 8):
            dy, dc = row[o]
            back = index_of(-dy, dc)
            send(pn.at[r, pl.ds(o * BR, BR)], rb.at[r, pl.ds(back * BR, BR)], ns.at[r, o - 1], nr.at[r, back - 1],
                 dev(dy=dy, dc=dc))
        rb[r, pl.ds(0, BR), :] = pn[r, pl.ds(0, BR), :]

    def grads(r):
        def part(n, _):
            cols = pl.ds(pl.multiple_of(n * 256, 256), 256)
            gf[r, :, cols] = dot(weights(r), psel[r, :, cols], 0, 0)
            return 0

        lax.fori_loop(0, 4, part, 0)

    def pass_on(side, h, i, add):
        mineb, came = (gsp, grp) if side == 0 else (gsm, grm)
        r = 4 - h if side == 0 else (4 + h) % 8
        value = gf[r, rows(i), :]
        if add:
            arrived(came.at[h - 1, rows(i)], gr.at[side, h - 1, i])
            value = value + came[h - 1, rows(i), :].astype(F32)
        mineb[h, rows(i), :] = value.astype(BF16)
        send(mineb.at[h, rows(i)], came.at[h, rows(i)], gs.at[side, h, i], gr.at[side, h, i],
             dev(dz=1 if side == 0 else NZ - 1))

    weights_arrived(4)
    weigh(1)
    panels(4)
    grads(4)
    for k in range(2):
        pass_on(0, 0, k, False)
        pass_on(1, 0, 2 + k, False)
    send_stats(1)
    weights_arrived(3)
    weigh(2)
    row_q_arrived(4)
    row_q_arrived(5)
    send_row_sib(2)
    weights_arrived(0)
    for o in range(1, 8):
        dy, dc = row[o]
        back = index_of(-dy, dc)
        for half in range(2):
            send(wt.at[0, half, pl.ds(o * BR, BR)], wrow.at[back, half], vs.at[o - 1, half], vr.at[back - 1, half], dev(dy=dy, dc=dc))
    for r in (3, 5):
        if r == 5:
            weights_arrived(r)
        panels(r)
        grads(r)
        for k in range(2):
            pass_on(0 if r == 3 else 1, 1, (2 + k) if r == 3 else k, False)
        weights_arrived((r + 4) % 8)
        panels((r + 4) % 8)
    for k in range(2):
        pass_on(0, 1, k, True)
        pass_on(1, 1, 2 + k, True)
    for r in (2, 6):
        weights_arrived(r)
        grads(r)
        panels(r)
    for h in range(2, 4):
        if h == 3:
            grads(1)
            grads(7)
        for k in range(4):
            pass_on(0, h, (k + 2) % 4, True)
            pass_on(1, h, k, True)
    grads(0)
    for d in range(1, NZ):
        arrived(stat.at[1, d], tr.at[1, d - 1])
    pos = jnp.zeros((4, 128), F32)
    for d in range(NZ):
        pos = pos + stat[1, d, 0:4]
    losses = (top - pos) + jnp.log(total)
    own_pair = lax.rem(z, 4)
    tile = jnp.zeros((1, 128), F32)
    for p in range(4):
        tile = jnp.where(own_pair == p, losses[p:p + 1], tile)
    lossb[x] = jnp.broadcast_to(tile, (8, 128))
    for d in range(1, NX):
        send(lossb.at[x], lossb.at[x], ls.at[d - 1], lr.at[3 - d], dev(dx=d))

    def row_panels():
        for a in range(NY):
            arrived(qrow.at[a, 1], fr.at[a])
        for j in range(8):
            dy, dc = row[j]
            if j:
                for half in range(2):
                    arrived(wrow.at[j, half], vr.at[j - 1, half])
            w = [wrow[j, half] if j else wt[0, half, 0:BR, :] for half in range(2)]
            w = jnp.concatenate(w, axis=1)
            q = qrow.at[dy, dc] if j else qb.at[0]
            rb[0, pl.ds(j * BR, BR), :] = dot(w, q[...], 1, 0).astype(BF16)

    def collect(r, first=False, last=False):
        if r:
            for j in range(1, 8):
                arrived(rb.at[r, pl.ds(j * BR, BR)], nr.at[r, j - 1])
        else:
            row_panels()

        for n in range(4):
            cols = pl.ds(n * 256, 256)
            term = dot(bback[r], rb[r, :, cols], 1, 0)
            term = term if first else acc[:, cols] + term
            if last:
                pg_ref[:, cols] = term.astype(BF16)
            else:
                acc[:, cols] = term

    for n, r in enumerate((4, 0, 3, 7, 5, 1, 2)):
        collect(r, first=n == 0)
    for k in range(4):
        ip, im = (k + 2) % 4, k
        arrived(grp.at[3, rows(ip)], gr.at[0, 3, ip])
        arrived(grm.at[3, rows(im)], gr.at[1, 3, im])
    for k in range(4):
        qg_ref[rows(k), :] = (gf[0, rows(k), :] + grp[3, rows(k), :].astype(F32) + grm[3, rows(k), :].astype(F32)).astype(BF16)
    for d in range(1, NX):
        other = lax.rem(x + d, NX)
        arrived(lossb.at[other], lr.at[d - 1])
    for half in range(2):
        loss_ref[half:half + 1, :] = lossb[z // 4 + 2 * half][0:1]
    for args, when in sent:
        if when is None:
            remote(*args).wait_send()
        else:
            @pl.when(when)
            def _():
                remote(*args).wait_send()
    collect(6, last=True)


def body(queries, passages, pos_ids, neg_ids, counts):
    dma = pltpu.SemaphoreType.DMA
    vm = pltpu.VMEM
    loss, query_grad, passage_grad = pl.pallas_call(
        kernel,
        out_shape=(pltpu.VMEM((2, 128), F32), pltpu.VMEM((QR, W), BF16), pltpu.VMEM((PR, W), BF16)),
        in_specs=[pl.BlockSpec(memory_space=pl.ANY)] * 5,
        out_specs=tuple([pl.BlockSpec(memory_space=pltpu.VMEM)] * 3),
        scratch_shapes=[
            vm((8, QR, W), BF16), vm((NY, NC, PR, W), BF16), vm((8, QR, W), BF16), vm((QR, PR), BF16), vm((8, PR, QR), BF16),
            vm((8, 16, 128), BF16), vm((8, 16, 128), BF16), vm((8, BR, 128), F32), vm((4, QR, 128), F32),
            vm((4, 4, QR, 128), F32), vm((4, 3, QR, 128), F32), vm((4, QR, 128), F32),
            vm((2, 8, 8, 128), F32), vm((8, 128), F32), vm((8, 2, QR, 128), BF16), vm((NX, 8, 128), F32),
            vm((8, QR, W), F32), vm((4, QR, W), BF16), vm((4, QR, W), BF16), vm((4, QR, W), BF16), vm((4, QR, W), BF16),
            vm((8, QR, W), BF16), vm((8, QR, W), BF16), vm((PR, W), F32),
            vm((NY, NC, QR, W), BF16), vm((8, 2, BR, 128), BF16),
            pltpu.SMEM((8,), jnp.int32), pltpu.SMEM((8, 7), jnp.int32), pltpu.SMEM((8,), jnp.int32),
            dma((5,)), dma((2, 14)), dma((2, 14)), dma((2, 12)), dma((2, 12)), dma((16,)), dma((16,)), dma((7,)), dma((7,)),
            dma((7,)), dma((7,)), dma((8, 3, 2)), dma((4, 3)), dma((2, 7)), dma((2, 7)), dma((4, 3)), dma((8, 2)),
            dma((3,)), dma((3,)), dma((2, 4, 4)), dma((2, 4, 4)), dma((8, 7)), dma((8, 7)), dma((2, 6)), dma((2, 6)), dma((4,)), dma((4,)),
            dma((7, 2)), dma((7, 2)),
        ],
        compiler_params=pltpu.CompilerParams(collective_id=0, has_side_effects=True, vmem_limit_bytes=60 * 2**20),
        cost_estimate=pl.CostEstimate(flops=10**10, bytes_accessed=4 * 10**6, transcendentals=10**6),
    )(pos_ids, neg_ids, counts, queries, passages)
    return loss.reshape(QR), query_grad, passage_grad


def solution(mesh):
    assert mesh.shape["dp"] == NZ * NY * NC and mesh.shape["mp"] == NX
    return jax.shard_map(
        body,
        mesh=mesh,
        in_specs=(P("dp", "mp"), P("dp", "mp"), P("dp"), P("dp", None), P("dp")),
        out_specs=(P("dp"), P("dp", "mp"), P("dp", "mp")),
        check_vma=False,
    )
```

```python
import jax
import jax.numpy as jnp
from jax import lax
from jax.experimental import pallas as pl
from jax.experimental.pallas import tpu as pltpu
from jax.sharding import PartitionSpec as P

D = 4096
BR = 32
NZ, NY, NC, NX = 8, 4, 2, 4
RY = (0, 1, 3, 2)
W = 1024
QR = 256
PR = 512
MESH = pl.DeviceIdType.MESH
F32 = jnp.float32
BF16 = jnp.bfloat16


def index_of(dy, dc):
    return RY.index(dy % NY) * NC + dc


def dot(a, b, ca, cb):
    return lax.dot_general(a, b, (((ca,), (cb,)), ((), ())), preferred_element_type=F32)


def kernel(pos_hbm, neg_hbm, cnt_hbm, q_hbm, p_hbm, loss_ref, qg_ref, pg_ref,
           qb, pb, psel, bsel, bback, meta, sels, selt, ask, st, srv, lg, stat, norm, wt, lossb,
           gf, gsp, gsm, grp, grm, pn, rb, acc, qrow, wrow, pos_ref, neg_ref, cnt_ref,
           lsem, qs, qr, ps, pr, sibs, sibr, ms, mr, es, er, ss, sr, ts, tr, ws, wr, ls, lr, gs, gr, ns, nr, ys, yr, fs, fr, vs, vr):
    dp = lax.axis_index("dp")
    x = lax.axis_index("mp")
    z = dp // (NY * NC)
    y = lax.rem(dp // NC, NY)
    c = lax.rem(dp, NC)
    xm, xh = lax.rem(x, 2), x // 2

    def dev(dz=0, dy=0, dc=0, dx=0):
        there = lax.rem(z + dz, NZ) * (NY * NC) + lax.rem(y + dy, NY) * NC + lax.rem(c + dc, NC)
        return (there, lax.rem(x + dx, NX))

    row = [(RY[o // NC], o % NC) for o in range(8)]
    peers = [dev(dz=d) for d in range(1, NZ)] + [dev(dy=a, dc=b) for a, b in row[1:]] + [dev(dx=d) for d in range(1, NX)]
    barrier = pltpu.get_barrier_semaphore()
    for p in peers:
        pl.semaphore_signal(barrier, 1, device_id=p, device_id_type=MESH)

    lists = [pltpu.make_async_copy(a, b, lsem.at[2 + n]) for n, (a, b) in enumerate(((pos_hbm, pos_ref), (neg_hbm, neg_ref), (cnt_hbm, cnt_ref)))]
    for one in lists:
        one.start()
    load_q = pltpu.make_async_copy(q_hbm, qb.at[0], lsem.at[0])
    load_p = pltpu.make_async_copy(p_hbm, pb.at[0, 0], lsem.at[1])
    load_q.start()
    load_p.start()

    sent = []

    def remote(src, dst, ssem, rsem, to):
        return pltpu.make_async_remote_copy(src_ref=src, dst_ref=dst, send_sem=ssem, recv_sem=rsem, device_id=to, device_id_type=MESH)

    def send(*args, when=None):
        if when is None:
            remote(*args).start()
        else:
            @pl.when(when)
            def _():
                remote(*args).start()
        sent.append((args, when))

    def arrived(dst, rsem):
        remote(dst, dst, rsem, rsem, peers[0]).wait_recv()

    def rows(i, n=64):
        return pl.ds(i * n, n)

    def send_q(k, j):
        i = k * 4 + j
        right, left = (q_hbm, q_hbm) if k == 0 else (qb.at[8 - k], qb.at[k])
        send(right.at[rows(j)], qb.at[7 - k, rows(j)], qs.at[0, i], qr.at[0, i], dev(dz=1))
        jm = (j + 2) % 4
        send(left.at[rows(jm)], qb.at[k + 1, rows(jm)], qs.at[1, i], qr.at[1, i], dev(dz=NZ - 1))

    def q_arrived(k, j):
        i = (k - 1) * 4 + j
        arrived(qb.at[8 - k, rows(j)], qr.at[0, i])
        arrived(qb.at[k, rows((j + 2) % 4)], qr.at[1, i])

    def send_row_q(t):
        up, down = (qb.at[0], qb.at[0]) if t < 4 else (qrow.at[3, 0], qrow.at[1, 0])
        a, b = (3, 1) if t < 4 else (2, 2)
        ip, im = (t, (t + 2) % 4) if t < 4 else (t - 4, t - 2)
        send(up.at[rows(ip)], qrow.at[a, 0, rows(ip)], ys.at[0, t], yr.at[0, t], dev(dy=1))
        send(down.at[rows(im)], qrow.at[b, 0, rows(im)], ys.at[1, t], yr.at[1, t], dev(dy=NY - 1))

    def row_q_arrived(t):
        a, b = (3, 1) if t < 4 else (2, 2)
        ip, im = (t, (t + 2) % 4) if t < 4 else (t - 4, t - 2)
        arrived(qrow.at[a, 0, rows(ip)], yr.at[0, t])
        arrived(qrow.at[b, 0, rows(im)], yr.at[1, t])

    def send_row_sib(a):
        send(qb.at[0] if a == 0 else qrow.at[a, 0], qrow.at[a, 1], fs.at[a], fr.at[a], dev(dc=1))

    def p_part(t):
        if t < 8:
            return t, (t + 4) % 8
        return t - 8, t - 4

    def send_p(t):
        ip, im = p_part(t)
        up, down = (p_hbm, p_hbm) if t < 8 else (pb.at[3, 0], pb.at[1, 0])
        a, b = (3, 1) if t < 8 else (2, 2)
        send(up.at[rows(ip)], pb.at[a, 0, rows(ip)], ps.at[0, t], pr.at[0, t], dev(dy=1))
        send(down.at[rows(im)], pb.at[b, 0, rows(im)], ps.at[1, t], pr.at[1, t], dev(dy=NY - 1))

    def send_sib(a, i, n, k):
        send((p_hbm if a == 0 else pb.at[a, 0]).at[rows(i, n)], pb.at[a, 1, rows(i, n)], sibs.at[k], sibr.at[k], dev(dc=1))

    def sib_arrived(a):
        if a == 2:
            for i in range(8):
                arrived(pb.at[2, 1, rows(i)], sibr.at[8 + i])
        else:
            for half in range(2):
                arrived(pb.at[a, 1, rows(half, 256)], sibr.at[2 * a + half])

    for one in lists:
        one.wait()
    lane = lax.broadcasted_iota(jnp.int32, (8, 128), 1)
    sub8 = lax.broadcasted_iota(jnp.int32, (8, 128), 0)
    o_l = lane & 7
    og = o_l >> 1
    ry_l = og ^ (og >> 1)
    owner = (((z + (lane >> 3)) & 7) << 3) + (((y + ry_l) & 3) << 1) + (c ^ (o_l & 1))
    owner = jnp.where(lane < 64, owner, -7)
    code = jnp.zeros((8, 128), jnp.int32)
    sel = jnp.full((8, 128), -1, jnp.int32)
    for s in range(8):
        col = jnp.full((8, 128), -1, jnp.int32)
        for b in range(8):
            block = pos_ref[b] if s == 0 else jnp.where(s - 1 < cnt_ref[b], neg_ref[b, s - 1], -1)
            col = jnp.where(sub8 == b, block, col)
        hit = (col >= 0) & ((col >> 4) == owner)
        code = jnp.where(hit, 2 if s == 0 else 1, code)
        sel = jnp.where(hit, col & 15, sel)
    sel = jnp.broadcast_to(jnp.max(sel, axis=0, keepdims=True), (8, 128))
    meta[0] = jnp.concatenate([code, sel], axis=0).astype(F32).astype(BF16)
    pl.semaphore_wait(barrier, len(peers))
    for d in range(1, NZ):
        send(meta.at[0], meta.at[8 - d], ms.at[d - 1], mr.at[7 - d], dev(dz=d))
    for j in range(4):
        send_q(0, j)
        send_p(j)
    for t in range(4, 8):
        send_p(t)
    send_sib(0, 0, 256, 0)
    send_sib(0, 1, 256, 1)

    def my_home(p):
        return lax.rem(p + 4 * xm - z + 8, 8)

    def take_lists():
        for r in range(1, NZ):
            arrived(meta.at[r], mr.at[r - 1])
        sub16 = lax.broadcasted_iota(jnp.int32, (16, 128), 0)
        table = jnp.zeros((16, 128), F32)
        for r in range(NZ):
            own = meta[r].astype(F32)[8:16]
            pair = jnp.concatenate([own, own], axis=0)
            table = jnp.where(sub16 == r, pair, table)
            for k in range(4):
                selt[r, pl.ds(8 * k, 8), :] = own * 32.0 + (sub8 + 8 * k).astype(F32)
        sels[0] = table.astype(BF16)
        for o in range(1, 8):
            dy, dc = row[o]
            back = index_of(-dy, dc)
            send(sels.at[0], sels.at[back], es.at[o - 1], er.at[back - 1], dev(dy=dy, dc=dc))
        for p in range(4):
            r = my_home(p)
            t = lax.rem(8 - r, 8)
            down = (lax.broadcasted_iota(jnp.int32, (QR, 128), 1)
                    == t * 8 + (lax.broadcasted_iota(jnp.int32, (QR, 128), 0) >> 5)).astype(F32).astype(BF16)
            across = (lax.broadcasted_iota(jnp.int32, (16, 128), 0)
                      == xh * 4 + (lax.broadcasted_iota(jnp.int32, (16, 128), 1) >> 5)).astype(F32).astype(BF16)
            ask[p] = dot(dot(down, meta[r], 1, 1).astype(BF16), across, 1, 0)

    jl = lax.broadcasted_iota(jnp.int32, (BR, PR), 1).astype(F32)

    def choose(o):
        for r in range(NZ):
            k = ((8 - r) % 8) * 8 + o
            want = jnp.broadcast_to(selt[r, :, k:k + 1], (BR, PR))
            bsel[o, pl.ds(r * BR, BR), :] = (want == jl).astype(F32).astype(BF16)

    def pick(o):
        dy, dc = row[o]

        def part(n, _):
            cols = pl.ds(pl.multiple_of(n * 256, 256), 256)
            got = dot(bsel[o], pb[dy, dc, :, cols], 1, 0).astype(BF16)
            for r in range(NZ):
                psel[r, pl.ds(o * BR, BR), cols] = got[r * BR:(r + 1) * BR]
            return 0

        lax.fori_loop(0, 4, part, 0)

    bounds = (0, 64, 192, 256)

    def score(r, gs_, halves):
        home = lax.rem(z + r, 8)
        p, m = lax.rem(home, 4), home // 4
        part = pl.ds(bounds[gs_[0]], bounds[gs_[-1] + 1] - bounds[gs_[0]])
        first, n = halves[0] * 128, len(halves) * 128
        got = dot(psel[r, part, :], qb[r, pl.ds(first, n), :], 1, 1)
        for half in halves:
            xt = m + 2 * half
            st[p, xt, part, :] = got[:, half * 128 - first:half * 128 - first + 128]
            slot = lax.rem(x - xt + 4, 4) - 1
            send(st.at[p, xt, part], srv.at[p, slot, part], ss.at[r, gs_[0], half], sr.at[p, slot], (dp, xt), when=xt != x)

    rowi = lax.broadcasted_iota(jnp.int32, (QR, 128), 0)
    lanei = lax.broadcasted_iota(jnp.int32, (QR, 128), 1)
    same_row = (rowi & 31) == (lanei & 31)

    def send_stats(n):
        for d in range(1, NZ):
            send(stat.at[n, 0], stat.at[n, 8 - d], ts.at[n, d - 1], tr.at[n, 7 - d], dev(dz=d))

    def row_stats():
        scale = jnp.zeros((8, 128), F32)
        hits = jnp.zeros((8, 128), F32)
        for n in (2, 1, 3, 0):
            p = lax.rem(z + n, 4)
            for k in range(3):
                arrived(srv.at[p, k], sr.at[p, k])
            summed = st[p, x] + srv[p, 0] + srv[p, 1] + srv[p, 2]
            live = ask[p] > 0.5
            logits = jnp.where(live, summed * (D ** -0.5), -1e30)
            lg[p] = logits
            top = jnp.max(logits, axis=0, keepdims=True)
            total = jnp.sum(jnp.where(live, jnp.exp(logits - top), 0.0), axis=0, keepdims=True)
            pos = jnp.sum(jnp.where((ask[p] > 1.5) & same_row, logits, 0.0), axis=0, keepdims=True)
            scale = jnp.where(sub8 == p, top, jnp.where(sub8 == 4 + p, total, scale))
            hits = jnp.where(sub8 == p, pos, hits)
        stat[0, 0] = scale
        stat[1, 0] = hits
        send_stats(0)

    def prepare(r):
        line = lax.broadcasted_iota(jnp.int32, (1, QR), 1)
        want = jnp.zeros((1, QR), F32)
        for j in range(8):
            dy, dc = row[j]
            k = ((8 - r) % 8) * 8 + index_of(-dy, dc)
            asked = jnp.broadcast_to(sels[j].astype(F32)[r:r + 1, k:k + 1], (1, QR))
            want = jnp.where((line >> 5) == j, asked * 32.0 + (line & 31).astype(F32), want)
        down = lax.broadcasted_iota(jnp.int32, (PR, QR), 0).astype(F32)
        bback[r] = (down == want).astype(F32).astype(BF16)

    here, scored = {(0, 0), (0, 1)}, set()

    def slot_events(t):
        k, j = t // 4 + 1, t % 4
        q_arrived(k, j)
        if k < 3 or (k == 3 and j < 2):
            send_q(k, j)
        if k == 4 and j == 1:
            here.update(((4, 0), (4, 1)))
        elif k < 4 and j % 2:
            here.update(((8 - k, j // 2), (k, 1 - j // 2)))
        if t < 12:
            ip, im = p_part(t)
            a, b = (3, 1) if t < 8 else (2, 2)
            arrived(pb.at[a, 0, rows(ip)], pr.at[0, t])
            arrived(pb.at[b, 0, rows(im)], pr.at[1, t])
            if t < 4:
                send_p(t + 8)
            if t == 3:
                send_sib(3, 0, 256, 6)
                send_sib(1, 1, 256, 3)
            if t == 7:
                send_sib(3, 1, 256, 7)
                send_sib(1, 0, 256, 2)
            if t > 7:
                send_sib(2, ip, 64, 8 + ip)
                send_sib(2, im, 64, 8 + im)

    def score_new(upto):
        for r in (1, 5, 2, 6, 3, 7, 0, 4):
            todo = {}
            for half in range(2):
                left = tuple(g for g in range(upto + 1) if (r, half) in here and (r, g, half) not in scored)
                if left:
                    todo.setdefault(left, []).append(half)
            for left, halves in todo.items():
                score(r, left, halves)
                scored.update((r, g, half) for g in left for half in halves)

    for t in range(14):
        slot_events(t)
        if t == 0:
            take_lists()
            load_q.wait()
            load_p.wait()
        if t == 1:
            choose(0)
            choose(1)
            pick(0)
        if 3 <= t < 7:
            choose(t - 1)
        if 8 <= t < 10:
            choose(t - 2)
        if t == 2:
            sib_arrived(0)
            pick(1)
        if t == 9:
            for o in range(1, 8):
                arrived(sels.at[o], er.at[o - 1])
        if 9 <= t < 11:
            prepare(2 * t - 18)
            prepare(2 * t - 17)
        if t == 7:
            pick(2)
            pick(4)
            sib_arrived(1)
            pick(3)
            sib_arrived(3)
            pick(5)
        if 2 <= t < 7:
            score_new(0)
        if 7 <= t < 12:
            score_new(1)
        if t == 11:
            pick(6)
            sib_arrived(2)
            pick(7)
            for n in range(4):
                send_row_q(n)
            send_row_sib(0)
        if t >= 11:
            score_new(2)
    for n in range(2):
        row_q_arrived(n)
        send_row_q(n + 4)
    assert len(scored) == 48
    row_stats()
    for r in range(4, 8):
        prepare(r)
    row_q_arrived(2)
    row_q_arrived(3)
    send_row_sib(1)
    send_row_sib(3)

    for d in range(1, NZ):
        arrived(stat.at[0, d], tr.at[0, d - 1])
    top = stat[0, 0, 0:4]
    for d in range(1, NZ):
        top = jnp.maximum(top, stat[0, d, 0:4])
    total = jnp.zeros((4, 128), F32)
    for d in range(NZ):
        total = total + stat[0, d, 4:8] * jnp.exp(stat[0, d, 0:4] - top)
    norm[0:4] = top
    norm[4:8] = 1.0 / total

    def weigh(s):
        p = lax.rem(z + s, 4)
        r = my_home(p)
        hot = jnp.where((ask[p] > 1.5) & same_row, 1.0, 0.0)
        wt[r, xh] = (jnp.exp(lg[p] - norm[pl.ds(p, 1), :]) * norm[pl.ds(4 + p, 1), :] - hot).astype(BF16)
        for d in range(1, NX):
            send(wt.at[r, xh], wt.at[r, xh], ws.at[s, d - 1], wr.at[r, xh], dev(dx=d))

    weigh(0)
    weigh(3)
    def weights_arrived(r):
        home = lax.rem(z + r, 8)
        for half in range(2):
            @pl.when(home // 4 + 2 * half != x)
            def _():
                arrived(wt.at[r, half], wr.at[r, half])

    def weights(r):
        return jnp.concatenate([wt[r, 0], wt[r, 1]], axis=1)

    def panels(r):
        def part(n, _):
            cols = pl.ds(pl.multiple_of(n * 256, 256), 256)
            pn[r, :, cols] = dot(weights(r), qb[r, :, cols], 1, 0).astype(BF16)
            return 0

        lax.fori_loop(0, 4, part, 0)
        for o in range(1, 8):
            dy, dc = row[o]
            back = index_of(-dy, dc)
            send(pn.at[r, pl.ds(o * BR, BR)], rb.at[r, pl.ds(back * BR, BR)], ns.at[r, o - 1], nr.at[r, back - 1],
                 dev(dy=dy, dc=dc))
        rb[r, pl.ds(0, BR), :] = pn[r, pl.ds(0, BR), :]

    def grads(r):
        def part(n, _):
            cols = pl.ds(pl.multiple_of(n * 256, 256), 256)
            gf[r, :, cols] = dot(weights(r), psel[r, :, cols], 0, 0)
            return 0

        lax.fori_loop(0, 4, part, 0)

    def pass_on(side, h, i, add):
        mineb, came = (gsp, grp) if side == 0 else (gsm, grm)
        r = 4 - h if side == 0 else (4 + h) % 8
        value = gf[r, rows(i), :]
        if add:
            arrived(came.at[h - 1, rows(i)], gr.at[side, h - 1, i])
            value = value + came[h - 1, rows(i), :].astype(F32)
        mineb[h, rows(i), :] = value.astype(BF16)
        send(mineb.at[h, rows(i)], came.at[h, rows(i)], gs.at[side, h, i], gr.at[side, h, i],
             dev(dz=1 if side == 0 else NZ - 1))

    weights_arrived(4)
    weigh(1)
    panels(4)
    grads(4)
    for k in range(2):
        pass_on(0, 0, k, False)
        pass_on(1, 0, 2 + k, False)
    send_stats(1)
    weights_arrived(3)
    weigh(2)
    row_q_arrived(4)
    row_q_arrived(5)
    send_row_sib(2)
    weights_arrived(0)
    for o in range(1, 8):
        dy, dc = row[o]
        back = index_of(-dy, dc)
        for half in range(2):
            send(wt.at[0, half, pl.ds(o * BR, BR)], wrow.at[back, half], vs.at[o - 1, half], vr.at[back - 1, half], dev(dy=dy, dc=dc))
    for r in (3, 5):
        if r == 5:
            weights_arrived(r)
        panels(r)
        grads(r)
        for k in range(2):
            pass_on(0 if r == 3 else 1, 1, (2 + k) if r == 3 else k, False)
        weights_arrived((r + 4) % 8)
        panels((r + 4) % 8)
    for k in range(2):
        pass_on(0, 1, k, True)
        pass_on(1, 1, 2 + k, True)
    for r in (2, 6):
        weights_arrived(r)
        grads(r)
        panels(r)
    for h in range(2, 4):
        if h == 3:
            grads(1)
            grads(7)
        for k in range(4):
            pass_on(0, h, (k + 2) % 4, True)
            pass_on(1, h, k, True)
    grads(0)
    for d in range(1, NZ):
        arrived(stat.at[1, d], tr.at[1, d - 1])
    pos = jnp.zeros((4, 128), F32)
    for d in range(NZ):
        pos = pos + stat[1, d, 0:4]
    losses = (top - pos) + jnp.log(total)
    own_pair = lax.rem(z, 4)
    tile = jnp.zeros((1, 128), F32)
    for p in range(4):
        tile = jnp.where(own_pair == p, losses[p:p + 1], tile)
    lossb[x] = jnp.broadcast_to(tile, (8, 128))
    for d in range(1, NX):
        send(lossb.at[x], lossb.at[x], ls.at[d - 1], lr.at[3 - d], dev(dx=d))

    def row_panels():
        for a in range(NY):
            arrived(qrow.at[a, 1], fr.at[a])
        for j in range(8):
            dy, dc = row[j]
            if j:
                for half in range(2):
                    arrived(wrow.at[j, half], vr.at[j - 1, half])
            w = [wrow[j, half] if j else wt[0, half, 0:BR, :] for half in range(2)]
            w = jnp.concatenate(w, axis=1)
            q = qrow.at[dy, dc] if j else qb.at[0]
            rb[0, pl.ds(j * BR, BR), :] = dot(w, q[...], 1, 0).astype(BF16)

    def collect(r, first=False, last=False):
        if r:
            for j in range(1, 8):
                arrived(rb.at[r, pl.ds(j * BR, BR)], nr.at[r, j - 1])
        else:
            row_panels()

        for n in range(4):
            cols = pl.ds(n * 256, 256)
            term = dot(bback[r], rb[r, :, cols], 1, 0)
            term = term if first else acc[:, cols] + term
            if last:
                pg_ref[:, cols] = term.astype(BF16)
            else:
                acc[:, cols] = term

    for n, r in enumerate((4, 0, 3, 7, 5, 1, 2)):
        collect(r, first=n == 0)
    for k in range(4):
        ip, im = (k + 2) % 4, k
        arrived(grp.at[3, rows(ip)], gr.at[0, 3, ip])
        arrived(grm.at[3, rows(im)], gr.at[1, 3, im])
    for k in range(4):
        qg_ref[rows(k), :] = (gf[0, rows(k), :] + grp[3, rows(k), :].astype(F32) + grm[3, rows(k), :].astype(F32)).astype(BF16)
    for d in range(1, NX):
        other = lax.rem(x + d, NX)
        arrived(lossb.at[other], lr.at[d - 1])
    for half in range(2):
        loss_ref[half:half + 1, :] = lossb[z // 4 + 2 * half][0:1]
    for args, when in sent:
        if when is None:
            remote(*args).wait_send()
        else:
            @pl.when(when)
            def _():
                remote(*args).wait_send()
    collect(6, last=True)


def body(queries, passages, pos_ids, neg_ids, counts):
    dma = pltpu.SemaphoreType.DMA
    vm = pltpu.VMEM
    loss, query_grad, passage_grad = pl.pallas_call(
        kernel,
        out_shape=(pltpu.VMEM((2, 128), F32), pltpu.VMEM((QR, W), BF16), pltpu.VMEM((PR, W), BF16)),
        in_specs=[pl.BlockSpec(memory_space=pl.ANY)] * 5,
        out_specs=tuple([pl.BlockSpec(memory_space=pltpu.VMEM)] * 3),
        scratch_shapes=[
            vm((8, QR, W), BF16), vm((NY, NC, PR, W), BF16), vm((8, QR, W), BF16), vm((8, QR, PR), BF16), vm((8, PR, QR), BF16),
            vm((8, 16, 128), BF16), vm((8, 16, 128), BF16), vm((8, BR, 128), F32), vm((4, QR, 128), F32),
            vm((4, 4, QR, 128), F32), vm((4, 3, QR, 128), F32), vm((4, QR, 128), F32),
            vm((2, 8, 8, 128), F32), vm((8, 128), F32), vm((8, 2, QR, 128), BF16), vm((NX, 8, 128), F32),
            vm((8, QR, W), F32), vm((4, QR, W), BF16), vm((4, QR, W), BF16), vm((4, QR, W), BF16), vm((4, QR, W), BF16),
            vm((8, QR, W), BF16), vm((8, QR, W), BF16), vm((PR, W), F32),
            vm((NY, NC, QR, W), BF16), vm((8, 2, BR, 128), BF16),
            pltpu.SMEM((8,), jnp.int32), pltpu.SMEM((8, 7), jnp.int32), pltpu.SMEM((8,), jnp.int32),
            dma((5,)), dma((2, 14)), dma((2, 14)), dma((2, 12)), dma((2, 12)), dma((16,)), dma((16,)), dma((7,)), dma((7,)),
            dma((7,)), dma((7,)), dma((8, 3, 2)), dma((4, 3)), dma((2, 7)), dma((2, 7)), dma((4, 3)), dma((8, 2)),
            dma((3,)), dma((3,)), dma((2, 4, 4)), dma((2, 4, 4)), dma((8, 7)), dma((8, 7)), dma((2, 6)), dma((2, 6)), dma((4,)), dma((4,)),
            dma((7, 2)), dma((7, 2)),
        ],
        compiler_params=pltpu.CompilerParams(collective_id=0, has_side_effects=True, vmem_limit_bytes=60 * 2**20),
        cost_estimate=pl.CostEstimate(flops=10**10, bytes_accessed=4 * 10**6, transcendentals=10**6),
    )(pos_ids, neg_ids, counts, queries, passages)
    return loss.reshape(QR), query_grad, passage_grad


def solution(mesh):
    assert mesh.shape["dp"] == NZ * NY * NC and mesh.shape["mp"] == NX
    return jax.shard_map(
        body,
        mesh=mesh,
        in_specs=(P("dp", "mp"), P("dp", "mp"), P("dp"), P("dp", None), P("dp")),
        out_specs=(P("dp"), P("dp", "mp"), P("dp", "mp")),
        check_vma=False,
    )
```

```python
import jax
import jax.numpy as jnp
from jax import lax
from jax.experimental import pallas as pl
from jax.experimental.pallas import tpu as pltpu
from jax.sharding import PartitionSpec as P

D = 4096
BR = 32
NZ, NY, NC, NX = 8, 4, 2, 4
RY = (0, 1, 3, 2)
W = 1024
QR = 256
FW = 384
PR = 512
MESH = pl.DeviceIdType.MESH
F32 = jnp.float32
BF16 = jnp.bfloat16


def index_of(dy, dc):
    return RY.index(dy % NY) * NC + dc


def dot(a, b, ca, cb):
    return lax.dot_general(a, b, (((ca,), (cb,)), ((), ())), preferred_element_type=F32)


def kernel(pos_hbm, neg_hbm, cnt_hbm, q_hbm, p_hbm, loss_ref, qg_ref, pg_ref,
           qb, pb, psel, bsel, bback, meta, sels, selt, ask, st, srv, lg, stat, norm, wt, lossb,
           gf, gsp, gsm, grp, grm, pn, rb, acc, qrow, wrow, qrow2, wrow2, pos_ref, neg_ref, cnt_ref,
           lsem, qs, qr, ps, pr, sibs, sibr, ms, mr, es, er, ss, sr, ts, tr, ws, wr, ls, lr, gs, gr, ns, nr, ys, yr, fs, fr, vs, vr, ys2, yr2, fs2, fr2, vs2, vr2):
    dp = lax.axis_index("dp")
    x = lax.axis_index("mp")
    z = dp // (NY * NC)
    y = lax.rem(dp // NC, NY)
    c = lax.rem(dp, NC)
    xm, xh = lax.rem(x, 2), x // 2

    def dev(dz=0, dy=0, dc=0, dx=0):
        there = lax.rem(z + dz, NZ) * (NY * NC) + lax.rem(y + dy, NY) * NC + lax.rem(c + dc, NC)
        return (there, lax.rem(x + dx, NX))

    row = [(RY[o // NC], o % NC) for o in range(8)]
    peers = [dev(dz=d) for d in range(1, NZ)] + [dev(dy=a, dc=b) for a, b in row[1:]] + [dev(dx=d) for d in range(1, NX)]
    barrier = pltpu.get_barrier_semaphore()
    for p in peers:
        pl.semaphore_signal(barrier, 1, device_id=p, device_id_type=MESH)

    lists = [pltpu.make_async_copy(a, b, lsem.at[2 + n]) for n, (a, b) in enumerate(((pos_hbm, pos_ref), (neg_hbm, neg_ref), (cnt_hbm, cnt_ref)))]
    for one in lists:
        one.start()
    load_q = pltpu.make_async_copy(q_hbm, qb.at[0], lsem.at[0])
    load_p = pltpu.make_async_copy(p_hbm, pb.at[0, 0], lsem.at[1])
    load_q.start()
    load_p.start()

    sent = []

    def remote(src, dst, ssem, rsem, to):
        return pltpu.make_async_remote_copy(src_ref=src, dst_ref=dst, send_sem=ssem, recv_sem=rsem, device_id=to, device_id_type=MESH)

    def send(*args, when=None):
        if when is None:
            remote(*args).start()
        else:
            @pl.when(when)
            def _():
                remote(*args).start()
        sent.append((args, when))

    def arrived(dst, rsem):
        remote(dst, dst, rsem, rsem, peers[0]).wait_recv()

    def rows(i, n=64):
        return pl.ds(i * n, n)

    def send_q(k, j):
        i = k * 4 + j
        right, left = (q_hbm, q_hbm) if k == 0 else (qb.at[8 - k], qb.at[k])
        send(right.at[rows(j)], qb.at[7 - k, rows(j)], qs.at[0, i], qr.at[0, i], dev(dz=1))
        jm = (j + 2) % 4
        send(left.at[rows(jm)], qb.at[k + 1, rows(jm)], qs.at[1, i], qr.at[1, i], dev(dz=NZ - 1))

    def q_arrived(k, j):
        i = (k - 1) * 4 + j
        arrived(qb.at[8 - k, rows(j)], qr.at[0, i])
        arrived(qb.at[k, rows((j + 2) % 4)], qr.at[1, i])

    def send_row_q(t):
        up, down = (qb.at[0], qb.at[0]) if t < 4 else (qrow.at[3, 0], qrow.at[1, 0])
        a, b = (3, 1) if t < 4 else (2, 2)
        ip, im = (t, (t + 2) % 4) if t < 4 else (t - 4, t - 2)
        send(up.at[rows(ip)], qrow.at[a, 0, rows(ip)], ys.at[0, t], yr.at[0, t], dev(dy=1))
        send(down.at[rows(im)], qrow.at[b, 0, rows(im)], ys.at[1, t], yr.at[1, t], dev(dy=NY - 1))

    def row_q_arrived(t):
        a, b = (3, 1) if t < 4 else (2, 2)
        ip, im = (t, (t + 2) % 4) if t < 4 else (t - 4, t - 2)
        arrived(qrow.at[a, 0, rows(ip)], yr.at[0, t])
        arrived(qrow.at[b, 0, rows(im)], yr.at[1, t])

    def send_row_sib(a):
        send(qb.at[0] if a == 0 else qrow.at[a, 0], qrow.at[a, 1], fs.at[a], fr.at[a], dev(dc=1))

    def send_row_q2(t):
        up, down = (qb.at[7, :, pl.ds(0, FW)], qb.at[7, :, pl.ds(0, FW)]) if t < 4 else (qrow2.at[3, 0], qrow2.at[1, 0])
        a, b = (3, 1) if t < 4 else (2, 2)
        ip, im = (t, (t + 2) % 4) if t < 4 else (t - 4, t - 2)
        send(up.at[rows(ip)], qrow2.at[a, 0, rows(ip)], ys2.at[0, t], yr2.at[0, t], dev(dy=1))
        send(down.at[rows(im)], qrow2.at[b, 0, rows(im)], ys2.at[1, t], yr2.at[1, t], dev(dy=NY - 1))

    def row_q2_arrived(t):
        a, b = (3, 1) if t < 4 else (2, 2)
        ip, im = (t, (t + 2) % 4) if t < 4 else (t - 4, t - 2)
        arrived(qrow2.at[a, 0, rows(ip)], yr2.at[0, t])
        arrived(qrow2.at[b, 0, rows(im)], yr2.at[1, t])

    def send_row_sib2(a):
        send(qb.at[7, :, pl.ds(0, FW)] if a == 0 else qrow2.at[a, 0], qrow2.at[a, 1], fs2.at[a], fr2.at[a], dev(dc=1))

    def p_part(t):
        if t < 8:
            return t, (t + 4) % 8
        return t - 8, t - 4

    def send_p(t):
        ip, im = p_part(t)
        up, down = (p_hbm, p_hbm) if t < 8 else (pb.at[3, 0], pb.at[1, 0])
        a, b = (3, 1) if t < 8 else (2, 2)
        send(up.at[rows(ip)], pb.at[a, 0, rows(ip)], ps.at[0, t], pr.at[0, t], dev(dy=1))
        send(down.at[rows(im)], pb.at[b, 0, rows(im)], ps.at[1, t], pr.at[1, t], dev(dy=NY - 1))

    def send_sib(a, i, n, k):
        send((p_hbm if a == 0 else pb.at[a, 0]).at[rows(i, n)], pb.at[a, 1, rows(i, n)], sibs.at[k], sibr.at[k], dev(dc=1))

    def sib_arrived(a):
        if a == 2:
            for i in range(8):
                arrived(pb.at[2, 1, rows(i)], sibr.at[8 + i])
        else:
            for half in range(2):
                arrived(pb.at[a, 1, rows(half, 256)], sibr.at[2 * a + half])

    for one in lists:
        one.wait()
    lane = lax.broadcasted_iota(jnp.int32, (8, 128), 1)
    sub8 = lax.broadcasted_iota(jnp.int32, (8, 128), 0)
    o_l = lane & 7
    og = o_l >> 1
    ry_l = og ^ (og >> 1)
    owner = (((z + (lane >> 3)) & 7) << 3) + (((y + ry_l) & 3) << 1) + (c ^ (o_l & 1))
    owner = jnp.where(lane < 64, owner, -7)
    code = jnp.zeros((8, 128), jnp.int32)
    sel = jnp.full((8, 128), -1, jnp.int32)
    for s in range(8):
        col = jnp.full((8, 128), -1, jnp.int32)
        for b in range(8):
            block = pos_ref[b] if s == 0 else jnp.where(s - 1 < cnt_ref[b], neg_ref[b, s - 1], -1)
            col = jnp.where(sub8 == b, block, col)
        hit = (col >= 0) & ((col >> 4) == owner)
        code = jnp.where(hit, 2 if s == 0 else 1, code)
        sel = jnp.where(hit, col & 15, sel)
    sel = jnp.broadcast_to(jnp.max(sel, axis=0, keepdims=True), (8, 128))
    meta[0] = jnp.concatenate([code, sel], axis=0).astype(F32).astype(BF16)
    pl.semaphore_wait(barrier, len(peers))
    for d in range(1, NZ):
        send(meta.at[0], meta.at[8 - d], ms.at[d - 1], mr.at[7 - d], dev(dz=d))
    for j in range(4):
        send_q(0, j)
        send_p(j)
    for t in range(4, 8):
        send_p(t)
    send_sib(0, 0, 256, 0)
    send_sib(0, 1, 256, 1)

    def my_home(p):
        return lax.rem(p + 4 * xm - z + 8, 8)

    def take_lists():
        for r in range(1, NZ):
            arrived(meta.at[r], mr.at[r - 1])
        sub16 = lax.broadcasted_iota(jnp.int32, (16, 128), 0)
        table = jnp.zeros((16, 128), F32)
        for r in range(NZ):
            own = meta[r].astype(F32)[8:16]
            pair = jnp.concatenate([own, own], axis=0)
            table = jnp.where(sub16 == r, pair, table)
            for k in range(4):
                selt[r, pl.ds(8 * k, 8), :] = own * 32.0 + (sub8 + 8 * k).astype(F32)
        sels[0] = table.astype(BF16)
        for o in range(1, 8):
            dy, dc = row[o]
            back = index_of(-dy, dc)
            send(sels.at[0], sels.at[back], es.at[o - 1], er.at[back - 1], dev(dy=dy, dc=dc))
        for p in range(4):
            r = my_home(p)
            t = lax.rem(8 - r, 8)
            down = (lax.broadcasted_iota(jnp.int32, (QR, 128), 1)
                    == t * 8 + (lax.broadcasted_iota(jnp.int32, (QR, 128), 0) >> 5)).astype(F32).astype(BF16)
            across = (lax.broadcasted_iota(jnp.int32, (16, 128), 0)
                      == xh * 4 + (lax.broadcasted_iota(jnp.int32, (16, 128), 1) >> 5)).astype(F32).astype(BF16)
            ask[p] = dot(dot(down, meta[r], 1, 1).astype(BF16), across, 1, 0)

    jl = lax.broadcasted_iota(jnp.int32, (BR, PR), 1).astype(F32)

    def choose(o):
        for r in range(NZ):
            k = ((8 - r) % 8) * 8 + o
            want = jnp.broadcast_to(selt[r, :, k:k + 1], (BR, PR))
            bsel[o, pl.ds(r * BR, BR), :] = (want == jl).astype(F32).astype(BF16)

    def pick(o):
        dy, dc = row[o]

        def part(n, _):
            cols = pl.ds(pl.multiple_of(n * 256, 256), 256)
            got = dot(bsel[o], pb[dy, dc, :, cols], 1, 0).astype(BF16)
            for r in range(NZ):
                psel[r, pl.ds(o * BR, BR), cols] = got[r * BR:(r + 1) * BR]
            return 0

        lax.fori_loop(0, 4, part, 0)

    bounds = (0, 64, 192, 256)

    def score(r, gs_, halves):
        home = lax.rem(z + r, 8)
        p, m = lax.rem(home, 4), home // 4
        part = pl.ds(bounds[gs_[0]], bounds[gs_[-1] + 1] - bounds[gs_[0]])
        first, n = halves[0] * 128, len(halves) * 128
        got = dot(psel[r, part, :], qb[r, pl.ds(first, n), :], 1, 1)
        for half in halves:
            xt = m + 2 * half
            st[p, xt, part, :] = got[:, half * 128 - first:half * 128 - first + 128]
            slot = lax.rem(x - xt + 4, 4) - 1
            send(st.at[p, xt, part], srv.at[p, slot, part], ss.at[r, gs_[0], half], sr.at[p, slot], (dp, xt), when=xt != x)

    rowi = lax.broadcasted_iota(jnp.int32, (QR, 128), 0)
    lanei = lax.broadcasted_iota(jnp.int32, (QR, 128), 1)
    same_row = (rowi & 31) == (lanei & 31)

    def send_stats(n):
        for d in range(1, NZ):
            send(stat.at[n, 0], stat.at[n, 8 - d], ts.at[n, d - 1], tr.at[n, 7 - d], dev(dz=d))

    def row_stats():
        scale = jnp.zeros((8, 128), F32)
        hits = jnp.zeros((8, 128), F32)
        for n in (2, 1, 3, 0):
            p = lax.rem(z + n, 4)
            for k in range(3):
                arrived(srv.at[p, k], sr.at[p, k])
            summed = st[p, x] + srv[p, 0] + srv[p, 1] + srv[p, 2]
            live = ask[p] > 0.5
            logits = jnp.where(live, summed * (D ** -0.5), -1e30)
            lg[p] = logits
            top = jnp.max(logits, axis=0, keepdims=True)
            total = jnp.sum(jnp.where(live, jnp.exp(logits - top), 0.0), axis=0, keepdims=True)
            pos = jnp.sum(jnp.where((ask[p] > 1.5) & same_row, logits, 0.0), axis=0, keepdims=True)
            scale = jnp.where(sub8 == p, top, jnp.where(sub8 == 4 + p, total, scale))
            hits = jnp.where(sub8 == p, pos, hits)
        stat[0, 0] = scale
        stat[1, 0] = hits
        send_stats(0)

    def prepare(r):
        line = lax.broadcasted_iota(jnp.int32, (1, QR), 1)
        want = jnp.zeros((1, QR), F32)
        for j in range(8):
            dy, dc = row[j]
            k = ((8 - r) % 8) * 8 + index_of(-dy, dc)
            asked = jnp.broadcast_to(sels[j].astype(F32)[r:r + 1, k:k + 1], (1, QR))
            want = jnp.where((line >> 5) == j, asked * 32.0 + (line & 31).astype(F32), want)
        down = lax.broadcasted_iota(jnp.int32, (PR, QR), 0).astype(F32)
        bback[r] = (down == want).astype(F32).astype(BF16)

    here, scored = {(0, 0), (0, 1)}, set()

    def slot_events(t):
        k, j = t // 4 + 1, t % 4
        q_arrived(k, j)
        if k < 3 or (k == 3 and j < 2):
            send_q(k, j)
        if k == 4 and j == 1:
            here.update(((4, 0), (4, 1)))
        elif k < 4 and j % 2:
            here.update(((8 - k, j // 2), (k, 1 - j // 2)))
        if t < 12:
            ip, im = p_part(t)
            a, b = (3, 1) if t < 8 else (2, 2)
            arrived(pb.at[a, 0, rows(ip)], pr.at[0, t])
            arrived(pb.at[b, 0, rows(im)], pr.at[1, t])
            if t < 4:
                send_p(t + 8)
            if t == 3:
                send_sib(3, 0, 256, 6)
                send_sib(1, 1, 256, 3)
            if t == 7:
                send_sib(3, 1, 256, 7)
                send_sib(1, 0, 256, 2)
            if t > 7:
                send_sib(2, ip, 64, 8 + ip)
                send_sib(2, im, 64, 8 + im)

    def score_new(upto):
        for r in (1, 5, 2, 6, 3, 7, 0, 4):
            todo = {}
            for half in range(2):
                left = tuple(g for g in range(upto + 1) if (r, half) in here and (r, g, half) not in scored)
                if left:
                    todo.setdefault(left, []).append(half)
            for left, halves in todo.items():
                score(r, left, halves)
                scored.update((r, g, half) for g in left for half in halves)

    for t in range(14):
        slot_events(t)
        if t == 0:
            take_lists()
            load_q.wait()
            load_p.wait()
        if t == 1:
            choose(0)
            choose(1)
            pick(0)
        if 3 <= t < 7:
            choose(t - 1)
        if 8 <= t < 10:
            choose(t - 2)
        if t == 2:
            sib_arrived(0)
            pick(1)
        if t == 9:
            for o in range(1, 8):
                arrived(sels.at[o], er.at[o - 1])
        if 9 <= t < 11:
            prepare(2 * t - 18)
            prepare(2 * t - 17)
        if t == 7:
            pick(2)
            pick(4)
            sib_arrived(1)
            pick(3)
            sib_arrived(3)
            pick(5)
        if 2 <= t < 7:
            score_new(0)
        if 7 <= t < 12:
            score_new(1)
        if t == 11:
            pick(6)
            sib_arrived(2)
            pick(7)
            for n in range(4):
                send_row_q(n)
            send_row_sib(0)
        if t >= 11:
            score_new(2)
    for n in range(2):
        row_q_arrived(n)
        send_row_q(n + 4)
    for n in range(4):
        send_row_q2(n)
    send_row_sib2(0)
    assert len(scored) == 48
    row_stats()
    for r in range(4, 8):
        prepare(r)
    row_q_arrived(2)
    row_q_arrived(3)
    send_row_sib(1)
    send_row_sib(3)

    for d in range(1, NZ):
        arrived(stat.at[0, d], tr.at[0, d - 1])
    top = stat[0, 0, 0:4]
    for d in range(1, NZ):
        top = jnp.maximum(top, stat[0, d, 0:4])
    total = jnp.zeros((4, 128), F32)
    for d in range(NZ):
        total = total + stat[0, d, 4:8] * jnp.exp(stat[0, d, 0:4] - top)
    norm[0:4] = top
    norm[4:8] = 1.0 / total

    def weigh(s):
        p = lax.rem(z + s, 4)
        r = my_home(p)
        hot = jnp.where((ask[p] > 1.5) & same_row, 1.0, 0.0)
        wt[r, xh] = (jnp.exp(lg[p] - norm[pl.ds(p, 1), :]) * norm[pl.ds(4 + p, 1), :] - hot).astype(BF16)
        for d in range(1, NX):
            send(wt.at[r, xh], wt.at[r, xh], ws.at[s, d - 1], wr.at[r, xh], dev(dx=d))

    weigh(0)
    weigh(3)
    for n in range(2):
        row_q2_arrived(n)
        send_row_q2(n + 4)
    def weights_arrived(r):
        home = lax.rem(z + r, 8)
        for half in range(2):
            @pl.when(home // 4 + 2 * half != x)
            def _():
                arrived(wt.at[r, half], wr.at[r, half])

    def weights(r):
        return jnp.concatenate([wt[r, 0], wt[r, 1]], axis=1)

    def panels(r):
        def part(n, _):
            cols = pl.ds(pl.multiple_of(n * 256, 256), 256)
            pn[r, :, cols] = dot(weights(r), qb[r, :, cols], 1, 0).astype(BF16)
            return 0

        lax.fori_loop(0, 4, part, 0)
        for o in range(1, 8):
            dy, dc = row[o]
            back = index_of(-dy, dc)
            cols = pl.ds(FW, W - FW) if r == 7 else pl.ds(0, W)
            send(pn.at[r, pl.ds(o * BR, BR), cols], rb.at[r, pl.ds(back * BR, BR), cols], ns.at[r, o - 1], nr.at[r, back - 1],
                 dev(dy=dy, dc=dc))
            for half in range(2 if r == 7 else 0):
                send(wt.at[7, half, pl.ds(o * BR, BR)], wrow2.at[back, half], vs2.at[o - 1, half], vr2.at[back - 1, half],
                     dev(dy=dy, dc=dc))
        rb[r, pl.ds(0, BR), :] = pn[r, pl.ds(0, BR), :]

    def grads(r):
        def part(n, _):
            cols = pl.ds(pl.multiple_of(n * 256, 256), 256)
            gf[r, :, cols] = dot(weights(r), psel[r, :, cols], 0, 0)
            return 0

        lax.fori_loop(0, 4, part, 0)

    def pass_on(side, h, i, add):
        mineb, came = (gsp, grp) if side == 0 else (gsm, grm)
        r = 4 - h if side == 0 else (4 + h) % 8
        value = gf[r, rows(i), :]
        if add:
            arrived(came.at[h - 1, rows(i)], gr.at[side, h - 1, i])
            value = value + came[h - 1, rows(i), :].astype(F32)
        mineb[h, rows(i), :] = value.astype(BF16)
        send(mineb.at[h, rows(i)], came.at[h, rows(i)], gs.at[side, h, i], gr.at[side, h, i],
             dev(dz=1 if side == 0 else NZ - 1))

    weights_arrived(4)
    weigh(1)
    panels(4)
    grads(4)
    for k in range(2):
        pass_on(0, 0, k, False)
        pass_on(1, 0, 2 + k, False)
    send_stats(1)
    weights_arrived(3)
    weigh(2)
    row_q_arrived(4)
    row_q_arrived(5)
    send_row_sib(2)
    row_q2_arrived(2)
    row_q2_arrived(3)
    send_row_sib2(1)
    send_row_sib2(3)
    weights_arrived(0)
    for o in range(1, 8):
        dy, dc = row[o]
        back = index_of(-dy, dc)
        for half in range(2):
            send(wt.at[0, half, pl.ds(o * BR, BR)], wrow.at[back, half], vs.at[o - 1, half], vr.at[back - 1, half], dev(dy=dy, dc=dc))
    for r in (3, 5):
        if r == 5:
            weights_arrived(r)
        panels(r)
        grads(r)
        for k in range(2):
            pass_on(0 if r == 3 else 1, 1, (2 + k) if r == 3 else k, False)
        weights_arrived((r + 4) % 8)
        panels((r + 4) % 8)
    for k in range(2):
        pass_on(0, 1, k, True)
        pass_on(1, 1, 2 + k, True)
    for r in (2, 6):
        weights_arrived(r)
        grads(r)
        panels(r)
    row_q2_arrived(4)
    row_q2_arrived(5)
    send_row_sib2(2)
    for h in range(2, 4):
        if h == 3:
            grads(1)
            grads(7)
        for k in range(4):
            pass_on(0, h, (k + 2) % 4, True)
            pass_on(1, h, k, True)
    grads(0)
    for d in range(1, NZ):
        arrived(stat.at[1, d], tr.at[1, d - 1])
    pos = jnp.zeros((4, 128), F32)
    for d in range(NZ):
        pos = pos + stat[1, d, 0:4]
    losses = (top - pos) + jnp.log(total)
    own_pair = lax.rem(z, 4)
    tile = jnp.zeros((1, 128), F32)
    for p in range(4):
        tile = jnp.where(own_pair == p, losses[p:p + 1], tile)
    lossb[x] = jnp.broadcast_to(tile, (8, 128))
    for d in range(1, NX):
        send(lossb.at[x], lossb.at[x], ls.at[d - 1], lr.at[3 - d], dev(dx=d))

    def row_panels():
        for a in range(NY):
            arrived(qrow.at[a, 1], fr.at[a])
        for j in range(8):
            dy, dc = row[j]
            if j:
                for half in range(2):
                    arrived(wrow.at[j, half], vr.at[j - 1, half])
            w = [wrow[j, half] if j else wt[0, half, 0:BR, :] for half in range(2)]
            w = jnp.concatenate(w, axis=1)
            q = qrow.at[dy, dc] if j else qb.at[0]
            rb[0, pl.ds(j * BR, BR), :] = dot(w, q[...], 1, 0).astype(BF16)

    def row_panels2():
        for a in range(NY):
            arrived(qrow2.at[a, 1], fr2.at[a])
        for j in range(1, 8):
            dy, dc = row[j]
            for half in range(2):
                arrived(wrow2.at[j, half], vr2.at[j - 1, half])
            w = jnp.concatenate([wrow2[j, 0], wrow2[j, 1]], axis=1)
            rb[7, pl.ds(j * BR, BR), pl.ds(0, FW)] = dot(w, qrow2[dy, dc], 1, 0).astype(BF16)

    def collect(r, first=False, last=False):
        if r:
            cols = pl.ds(FW, W - FW) if r == 7 else pl.ds(0, W)
            for j in range(1, 8):
                arrived(rb.at[r, pl.ds(j * BR, BR), cols], nr.at[r, j - 1])
            if r == 7:
                row_panels2()
        else:
            row_panels()

        for n in range(4):
            cols = pl.ds(n * 256, 256)
            term = dot(bback[r], rb[r, :, cols], 1, 0)
            term = term if first else acc[:, cols] + term
            if last:
                pg_ref[:, cols] = term.astype(BF16)
            else:
                acc[:, cols] = term

    for n, r in enumerate((4, 0, 3, 7, 5, 1, 2)):
        collect(r, first=n == 0)
    for k in range(4):
        ip, im = (k + 2) % 4, k
        arrived(grp.at[3, rows(ip)], gr.at[0, 3, ip])
        arrived(grm.at[3, rows(im)], gr.at[1, 3, im])
    for k in range(4):
        qg_ref[rows(k), :] = (gf[0, rows(k), :] + grp[3, rows(k), :].astype(F32) + grm[3, rows(k), :].astype(F32)).astype(BF16)
    for d in range(1, NX):
        other = lax.rem(x + d, NX)
        arrived(lossb.at[other], lr.at[d - 1])
    for half in range(2):
        loss_ref[half:half + 1, :] = lossb[z // 4 + 2 * half][0:1]
    for args, when in sent:
        if when is None:
            remote(*args).wait_send()
        else:
            @pl.when(when)
            def _():
                remote(*args).wait_send()
    collect(6, last=True)


def body(queries, passages, pos_ids, neg_ids, counts):
    dma = pltpu.SemaphoreType.DMA
    vm = pltpu.VMEM
    loss, query_grad, passage_grad = pl.pallas_call(
        kernel,
        out_shape=(pltpu.VMEM((2, 128), F32), pltpu.VMEM((QR, W), BF16), pltpu.VMEM((PR, W), BF16)),
        in_specs=[pl.BlockSpec(memory_space=pl.ANY)] * 5,
        out_specs=tuple([pl.BlockSpec(memory_space=pltpu.VMEM)] * 3),
        scratch_shapes=[
            vm((8, QR, W), BF16), vm((NY, NC, PR, W), BF16), vm((8, QR, W), BF16), vm((8, QR, PR), BF16), vm((8, PR, QR), BF16),
            vm((8, 16, 128), BF16), vm((8, 16, 128), BF16), vm((8, BR, 128), F32), vm((4, QR, 128), F32),
            vm((4, 4, QR, 128), F32), vm((4, 3, QR, 128), F32), vm((4, QR, 128), F32),
            vm((2, 8, 8, 128), F32), vm((8, 128), F32), vm((8, 2, QR, 128), BF16), vm((NX, 8, 128), F32),
            vm((8, QR, W), F32), vm((4, QR, W), BF16), vm((4, QR, W), BF16), vm((4, QR, W), BF16), vm((4, QR, W), BF16),
            vm((8, QR, W), BF16), vm((8, QR, W), BF16), vm((PR, W), F32),
            vm((NY, NC, QR, W), BF16), vm((8, 2, BR, 128), BF16), vm((NY, NC, QR, FW), BF16), vm((8, 2, BR, 128), BF16),
            pltpu.SMEM((8,), jnp.int32), pltpu.SMEM((8, 7), jnp.int32), pltpu.SMEM((8,), jnp.int32),
            dma((5,)), dma((2, 14)), dma((2, 14)), dma((2, 12)), dma((2, 12)), dma((16,)), dma((16,)), dma((7,)), dma((7,)),
            dma((7,)), dma((7,)), dma((8, 3, 2)), dma((4, 3)), dma((2, 7)), dma((2, 7)), dma((4, 3)), dma((8, 2)),
            dma((3,)), dma((3,)), dma((2, 4, 4)), dma((2, 4, 4)), dma((8, 7)), dma((8, 7)), dma((2, 6)), dma((2, 6)), dma((4,)), dma((4,)),
            dma((7, 2)), dma((7, 2)), dma((2, 6)), dma((2, 6)), dma((4,)), dma((4,)), dma((7, 2)), dma((7, 2)),
        ],
        compiler_params=pltpu.CompilerParams(collective_id=0, has_side_effects=True, vmem_limit_bytes=60 * 2**20),
        cost_estimate=pl.CostEstimate(flops=10**10, bytes_accessed=4 * 10**6, transcendentals=10**6),
    )(pos_ids, neg_ids, counts, queries, passages)
    return loss.reshape(QR), query_grad, passage_grad


def solution(mesh):
    assert mesh.shape["dp"] == NZ * NY * NC and mesh.shape["mp"] == NX
    return jax.shard_map(
        body,
        mesh=mesh,
        in_specs=(P("dp", "mp"), P("dp", "mp"), P("dp"), P("dp", None), P("dp")),
        out_specs=(P("dp"), P("dp", "mp"), P("dp", "mp")),
        check_vma=False,
    )
```
